256 devices in a mesh: leaf: 256 (over z, x, y, core).
Axes of the slice: x: 4, y: 4, z: 8, core: 2. Of those that a mesh axis runs over, the one named last changes fastest.
Arguments:
- densities: float32 [16, 524288], P(None, 'leaf'), may hold values from -6 to 6
- panels: float32 [3, 524288], P(None, 'leaf'), may hold values from -4 to 4
- areas: float32 [524288], P('leaf'), may hold values from 0.1 to 1
- near_offsets: int32 [8192, 6], P('leaf'), may hold values from -4 to 4, as said below
- near_count: int32 [8192], P('leaf'), may hold values from 1 to 6, as said below
- leaf_basis: float32 [8192, 64, 64], P('leaf'), may hold values from -0.25 to 0.25
- local_trans: float32 [15872, 64, 64], P('leaf'), may hold values from -0.625 to 0.625
- local_coupling: float32 [15872, 64, 64], P('leaf'), may hold values from -0.75 to 0.75
- up_trans: float32 [256, 8, 64, 64], P('leaf'), as said below
- coupling: float32 [256, 8, 64, 64], P('leaf'), as said below
Outputs:
- potential: float32 [16, 524288], P(None, 'leaf')
The draws below stay inside these ranges and needn't reach their ends.
Inputs may be any that keep to these rules, and one draw needn't show every extreme that they name: `near_offsets`: each row lists distinct offsets, the first is 0 (the leaf itself). Only the first near_count slots of a leaf's list are used; the first leaf of every device uses all 6. `up_trans`: entries are equal on all devices of one level-k cluster. `coupling`: entries are equal on all devices of one level-k cluster.
All inputs are finite; a program needn't handle non-finite values.
Results may differ from the reference program's by a relative error of at most 0.0003.
Values sent between devices are 32-bit elements; how exact they have to be, the bound alone decides.
A program may use at most 128 MiB of HBM per device.

```python
import math
import jax
import jax.numpy as jnp
from jax import lax

LEAF = 64
RANK = 64
RHS = 16
LEAVES_DEV = 32
HALO_LEAVES = 4
NNEAR = 6
LEVELS = 8
NODES = 256
LEAVES = 8192
UNKNOWNS = 524288


def tree_levels(key, scale):
    parts = []
    for level in range(LEVELS):
        sub = jax.random.fold_in(key, level)
        base = jax.random.normal(sub, (NODES // 2 ** level, RANK, RANK), jnp.float32) * scale
        parts.append(jnp.repeat(base, 2 ** level, axis=0))
    return jnp.stack(parts, 1)


def draw_up_trans(key, part):
    key = jax.random.fold_in(key, 11)
    return tree_levels(key, (2.0 * RANK) ** (-0.5))


def draw_coupling(key, part):
    key = jax.random.fold_in(key, 12)
    return tree_levels(key, RANK ** (-0.5))


def draw_near_offsets(key, part):
    key = jax.random.fold_in(key, 21)
    table = jnp.concatenate([jnp.arange(-HALO_LEAVES, 0, dtype=jnp.int32), jnp.arange(1, HALO_LEAVES + 1, dtype=jnp.int32)])
    keys = jax.random.split(key, LEAVES)
    rows = jax.vmap(lambda sub: jax.random.permutation(sub, table))(keys)[:, :NNEAR - 1]
    return jnp.concatenate([jnp.zeros((LEAVES, 1), jnp.int32), rows], 1)


def draw_near_count(key, part):
    key = jax.random.fold_in(key, 22)
    counts = jax.random.randint(key, (LEAVES,), 1, NNEAR + 1, dtype=jnp.int32)
    return counts.at[::LEAVES_DEV].set(NNEAR)


def block_levels(key, shape, pieces, least, high):
    factor_of, own = 1.0, jax.random.fold_in(key, 6)
    for axis_at, blocks in pieces:
        heights = jnp.exp(jax.random.uniform(jax.random.fold_in(own, axis_at), (blocks,), jnp.float32, least / len(pieces), high / len(pieces)))
        factor_of = factor_of * jnp.repeat(heights, shape[axis_at] // blocks).reshape([-1 if axis == axis_at else 1 for axis in range(len(shape))])
    return factor_of


def gaussian(key, extent, scale, reach, cuts=(), kind=jnp.bfloat16):
    result = scale * jax.random.normal(key, extent, jnp.float32)
    if cuts:
        result = result * block_levels(key, extent, cuts, -0.22, 0.18)
    return jnp.clip(result, -reach, reach).astype(kind)


def setup_inputs(seed: int = 0) -> dict:
    seeds = jax.random.split(jax.random.key(seed), 11)
    return {
        "densities": gaussian(seeds[0], (RHS, UNKNOWNS), 1.0, 6.0, ((1, 256),), jnp.float32),
        "panels": gaussian(seeds[1], (3, UNKNOWNS), 1.0, 4.0, ((1, 256),), jnp.float32),
        "areas": jnp.clip(jnp.exp(math.log(1.0) - 2.3025851 * jax.random.uniform(seeds[2], (UNKNOWNS,), jnp.float32) ** block_levels(seeds[2], (UNKNOWNS,), ((0, 256),), -0.2, 0.2)), 0.1, 1.0),
        "near_offsets": draw_near_offsets(jax.random.fold_in(seeds[10], 71), 0),
        "near_count": draw_near_count(jax.random.fold_in(seeds[10], 71), 0),
        "leaf_basis": gaussian(seeds[5], (LEAVES, LEAF, RANK), (8 * RANK) ** -0.5, 0.25, ((0, 256),), jnp.float32),
        "local_trans": gaussian(seeds[6], (2 * LEAVES - 2 * NODES, RANK, RANK), (3 * RANK // 2) ** -0.5, 0.625, ((0, 256),), jnp.float32),
        "local_coupling": gaussian(seeds[7], (2 * LEAVES - 2 * NODES, RANK, RANK), RANK ** -0.5, 0.75, ((0, 256),), jnp.float32),
        "up_trans": draw_up_trans(jax.random.fold_in(seeds[10], 71), 0),
        "coupling": draw_coupling(jax.random.fold_in(seeds[10], 71), 0),
    }


softening = 0.25
highest = lax.Precision.HIGHEST

def near_block(padded, offsets, counts, points):
    rows = padded.shape[0]
    leaves = offsets.shape[0]
    blocks = padded.reshape(rows, -1, LEAF)
    index = (offsets + HALO_LEAVES + jnp.arange(leaves, dtype=jnp.int32)[:, None]).astype(jnp.int32)
    source = jnp.take(blocks, index.reshape(-1), axis=1).reshape(rows, leaves, NNEAR * LEAF)
    live = (jnp.arange(NNEAR, dtype=jnp.int32)[None, :] < counts[:, None]).astype(jnp.float32)
    live = jnp.repeat(live, LEAF, axis=1)
    target = points.reshape(3, leaves, LEAF)
    dist = jnp.zeros((leaves, LEAF, NNEAR * LEAF), jnp.float32)
    for comp in range(3):
        delta = target[comp][:, :, None] - source[comp][:, None, :]
        dist = dist + delta * delta
    tile = (source[3] * live)[:, None, :] * lax.rsqrt(dist + softening)
    return jnp.einsum('iab,rib->ria', tile, source[4:], precision=highest)

def reference(densities, panels, areas, near_offsets, near_count, leaf_basis, local_trans, local_coupling, up_trans, coupling):
    width = HALO_LEAVES * LEAF
    stacked = jnp.concatenate([panels, areas[None, :], densities], 0)
    padded = jnp.pad(stacked, ((0, 0), (width, width)))
    offsets = near_offsets.reshape(NODES, LEAVES_DEV, NNEAR)
    counts = near_count.reshape(NODES, LEAVES_DEV)
    span = LEAVES_DEV * LEAF

    def one_device(dev):
        window = lax.dynamic_slice_in_dim(padded, dev * span, span + 2 * width, 1)
        points = lax.dynamic_slice_in_dim(panels, dev * span, span, 1)
        return near_block(window, offsets[dev], counts[dev], points)
    near = lax.map(one_device, jnp.arange(NODES, dtype=jnp.int32))
    near = jnp.transpose(near, (1, 0, 2, 3))
    depth = LEAVES_DEV.bit_length() - 1
    ltrans = local_trans.reshape(NODES, 2 * LEAVES_DEV - 2, RANK, RANK)
    lcouple = local_coupling.reshape(NODES, 2 * LEAVES_DEV - 2, RANK, RANK)
    basis = leaf_basis.reshape(NODES, LEAVES_DEV, LEAF, RANK)
    leafx = densities.reshape(RHS, NODES, LEAVES_DEV, LEAF)
    moments = jnp.einsum('dilk,rdil->dikr', basis, leafx, precision=highest)
    nearfar = []
    for level in range(depth):
        count = LEAVES_DEV >> level
        start = 2 * LEAVES_DEV - 2 * count
        transfer = ltrans[:, start:start + count]
        couple = lcouple[:, start:start + count]
        sibling = moments.reshape(NODES, count // 2, 2, RANK, RHS)[:, :, ::-1].reshape(moments.shape)
        nearfar.append(jnp.einsum('dnab,dnbr->dnar', couple, sibling, precision=highest))
        lifted = jnp.einsum('dnba,dnbr->dnar', transfer, moments, precision=highest)
        moments = lifted.reshape(NODES, count // 2, 2, RANK, RHS).sum(2)
    coef = moments[:, 0]
    farlist = []
    for level in range(LEVELS):
        trans = up_trans[::2 ** level, level]
        couple = coupling[::2 ** level, level]
        sibling = coef.reshape(-1, 2, RANK, RHS)[:, ::-1].reshape(coef.shape)
        farlist.append(jnp.einsum('nab,nbr->nar', couple, sibling, precision=highest))
        if level + 1 < LEVELS:
            lifted = jnp.einsum('nba,nbr->nar', trans, coef, precision=highest)
            coef = lifted.reshape(-1, 2, RANK, RHS).sum(1)
    local = farlist[LEVELS - 1]
    for level in range(LEVELS - 1, 0, -1):
        trans = up_trans[::2 ** (level - 1), level - 1]
        local = farlist[level - 1] + jnp.einsum('nab,nbr->nar', trans, jnp.repeat(local, 2, axis=0), precision=highest)
    downward = local[:, None]
    for level in range(depth - 1, -1, -1):
        count = LEAVES_DEV >> level
        start = 2 * LEAVES_DEV - 2 * count
        transfer = ltrans[:, start:start + count]
        downward = nearfar[level] + jnp.einsum('dnab,dnbr->dnar', transfer, jnp.repeat(downward, 2, axis=1), precision=highest)
    far = jnp.einsum('dilk,dikr->rdil', basis, downward, precision=highest)
    return (near + far).reshape(RHS, UNKNOWNS)
```

```python
import jax
import jax.numpy as jnp
from jax import lax
from jax.experimental import pallas as pl
from jax.experimental.pallas import tpu as pltpu
from jax.sharding import PartitionSpec as P

LEAF = 64
RANK = 64
RHS = 16
LEAVES = 32
HALO = 4
NNEAR = 6
LEVELS = 8
DEPTH = 5
NODES = 256
SPAN = LEAVES * LEAF
softening = 0.25
MESH = pl.DeviceIdType.MESH
f32 = jnp.float32
bf16 = jnp.bfloat16

PHASES = ((0, 3), (3, 2), (5, 3))
START = [2 * LEAVES - 2 * (LEAVES >> j) for j in range(DEPTH)]
PAIR = [s // 2 for s in START]


def split(x):
    high = x.astype(bf16)
    return high, (x - high.astype(f32)).astype(bf16)


def dot(a, b):
    return lax.dot_general(a, b, (((1,), (0,)), ((), ())), preferred_element_type=f32)


def dot_t(a, b):
    return lax.dot_general(a, b, (((1,), (1,)), ((), ())), preferred_element_type=f32)


def product(a, b, op):
    ah, al = a
    bh, bl = b
    rows = ah.shape[0]
    both = op(jnp.concatenate([ah, al], 0), bh)
    return both[:rows] + (both[rows:] + op(ah, bl))


def sweep(count, body, unroll):
    if count <= unroll:
        for i in range(count):
            body(i)
        return

    def step(i, carry):
        for u in range(unroll):
            body(i * unroll + u)
        return carry

    lax.fori_loop(0, count // unroll, step, 0)


def rows_at(index, count):
    if isinstance(index, int):
        return slice(index * count, (index + 1) * count)
    return pl.ds(pl.multiple_of(index * count, count), count)


def kernel(
    dens_hbm, pan_hbm, area_hbm, off_ref, cnt_ref, bas_hbm, ltr_hbm, lco_hbm, upt_hbm, cpl_hbm,
    out_ref,
    dens, pan, area, bas, ltr, lco, upt, cpl,
    bas_h, bas_l, ltr_h, ltr_l, gch, gcl, dh, dl,
    blocks, points, qrow, gpair, hpair, acc,
    wt1h, wt1l, wt2h, wt2l, wt3h, wt3l, wk_h, wk_l,
    send, recv, load_sem, send_sem, recv_sem, halo_ssem, halo_rsem,
):
    me = lax.axis_index("leaf")
    right = lax.rem(me + 1, NODES)
    left = lax.rem(me + NODES - 1, NODES)
    barrier = pltpu.get_barrier_semaphore()
    peers = [p << first for first, levels in PHASES for p in range(1, 1 << levels)]
    for p in peers:
        pl.semaphore_signal(barrier, inc=1, device_id=(me ^ p,), device_id_type=MESH)
    for neighbour in (left, right):
        pl.semaphore_signal(barrier, inc=1, device_id=(neighbour,), device_id_type=MESH)

    loads = {}
    for at, (name, src, dst) in enumerate(
        (
            ("dens", dens_hbm, dens),
            ("bas", bas_hbm, bas),
            ("ltr", ltr_hbm, ltr),
            ("upt", upt_hbm, upt),
            ("pan", pan_hbm, pan),
            ("area", area_hbm, area),
            ("lco", lco_hbm, lco),
            ("cpl", cpl_hbm, cpl),
        )
    ):
        loads[name] = pltpu.make_async_copy(src, dst, load_sem.at[at])
        loads[name].start()

    lane = lax.broadcasted_iota(jnp.int32, (1, 2 * LEAF), 1)
    low = lane < LEAF
    half = jnp.zeros((RHS, LEAF), f32)

    loads["dens"].wait()
    loads["bas"].wait()

    def moments(p):
        x = dens[:, rows_at(p, 2 * LEAF)]
        x = jnp.concatenate([jnp.where(low, x, 0.0), jnp.where(low, 0.0, x)], 0)
        w = split(bas[rows_at(p, 2)].reshape(2 * LEAF, RANK))
        bas_h[rows_at(p, 2 * LEAF)] = w[0]
        bas_l[rows_at(p, 2 * LEAF)] = w[1]
        qrow[p] = product(split(x), w, dot)

    sweep(LEAVES // 2, moments, 4)
    loads["ltr"].wait()

    def lift(level, p):
        q = qrow[PAIR[level] + p]
        q = jnp.concatenate([q[:RHS], q[RHS:]], 1)
        at = PAIR[level] + p
        w = split(ltr[rows_at(at, 2)].reshape(2 * RANK, RANK))
        ltr_h[rows_at(at, 2 * RANK)] = w[0]
        ltr_l[rows_at(at, 2 * RANK)] = w[1]
        return product(split(q), w, dot)

    for level in range(DEPTH - 1):

        def lift_two(m, level=level):
            qrow[PAIR[level + 1] + m] = jnp.concatenate(
                [lift(level, 2 * m), lift(level, 2 * m + 1)], 0
            )

        sweep(LEAVES >> (level + 2), lift_two, 4)
    loads["upt"].wait()

    e = [split(upt[0, k]) for k in range(LEVELS - 1)]
    zero = jnp.zeros((RANK, RANK), f32)

    def chain(first, count):
        out = [upt[0, first]]
        for k in range(first + 1, first + count):
            out.append(product(split(out[-1]), e[k], dot))
        return out

    t1, t2, t3 = chain(0, 3)
    wt1h[...], wt1l[...] = split(jnp.concatenate([t3, zero, t3, t1, t3, t2], 1))
    coef = lift(DEPTH - 1, 0)

    def exchange(phase, messages):
        first, levels = PHASES[phase]
        base = sum((1 << n) - 1 for _, n in PHASES[:phase])
        slot = sum(n for _, n in PHASES[:phase])
        for k in range(levels):
            send[slot + k] = messages[k]
        copies = []
        for p in reversed(range(1, 1 << levels)):
            copy = pltpu.make_async_remote_copy(
                src_ref=send.at[slot + p.bit_length() - 1],
                dst_ref=recv.at[base + p - 1],
                send_sem=send_sem.at[base + p - 1],
                recv_sem=recv_sem.at[base + p - 1],
                device_id=(me ^ (p << first),),
                device_id_type=MESH,
            )
            copy.start()
            copies.append(copy)

        def receive():
            for copy in copies:
                copy.wait()
            sums = []
            for k in range(levels):
                parts = [recv[base + p - 1] for p in range(1 << k, 2 << k)]
                while len(parts) > 1:
                    parts = [a + b for a, b in zip(parts[::2], parts[1::2])]
                sums.append(parts[0])
            return sums

        return receive

    own = product(split(coef), (wt1h[...], wt1l[...]), dot)
    own = [own[:, 2 * RANK * k : 2 * RANK * (k + 1)] for k in range(3)]
    own[0] = own[0] + jnp.concatenate([half, coef], 1)
    pl.semaphore_wait(barrier, len(peers) + 2)
    receive = exchange(0, own)

    loads["pan"].wait()
    loads["area"].wait()
    halo_rows = jnp.zeros((5, 2 * LEAF), f32)

    def pack(p):
        at = rows_at(p, 2 * LEAF)
        coords = jnp.concatenate([pan[:, at], halo_rows], 0)
        tile = jnp.concatenate([dens[:, at] * area[:, at], coords], 0)
        blocks[HALO + 2 * p] = tile
        blocks[HALO + 2 * p + 1] = pltpu.roll(tile, LEAF, 1)
        points[at, :] = coords.T

    sweep(LEAVES // 2, pack, 4)
    halos = []
    for at, (source, target, device) in enumerate(
        ((LEAVES, 0, right), (HALO, HALO + LEAVES, left))
    ):
        copy = pltpu.make_async_remote_copy(
            src_ref=blocks.at[pl.ds(source, HALO)],
            dst_ref=blocks.at[pl.ds(target, HALO)],
            send_sem=halo_ssem.at[at],
            recv_sem=halo_rsem.at[at],
            device_id=(device,),
            device_id_type=MESH,
        )
        copy.start()
        halos.append(copy)

    u4, u5 = chain(3, 2)
    wt2h[...], wt2l[...] = split(jnp.concatenate([u5, zero, u5, u4], 1))
    v6, v7 = chain(5, 2)
    wt3h[...], wt3l[...] = split(jnp.concatenate([zero, v6, v7, zero], 1))
    loads["cpl"].wait()
    t4 = product(split(t3), e[3], dot)
    t5 = product(split(t3), split(u5), dot)
    t6 = product(split(t5), e[5], dot)
    t7 = product(split(t5), split(v7), dot)
    blank = jnp.zeros((RANK, RANK), bf16)
    wk_h[:, rows_at(LEVELS, RANK)] = blank
    wk_l[:, rows_at(LEVELS, RANK)] = blank
    for k, t in enumerate((None, t1, t2, t3, t4, t5, t6, t7)):
        w = cpl[0, k] if t is None else product(split(t), split(cpl[0, k]), dot)
        wk_h[:, rows_at(k, RANK)], wk_l[:, rows_at(k, RANK)] = split(w)

    loads["lco"].wait()

    def couple(p):
        q = qrow[p]
        q = jnp.concatenate([q[RHS:], q[:RHS]], 0)
        w = split(lco[rows_at(p, 2)].reshape(2 * RANK, RANK))
        g = product(split(q), w, dot_t)
        gpair[p] = jnp.where(low, g[:RHS], g[RHS:])

    sweep(28, couple, 4)
    for p in range(28, 31):
        couple(p)

    sums = receive()
    tot = own[0] + (sums[0] + (sums[1] + sums[2]))
    coef = tot[:, :RANK]
    early = [s[:, RANK:] for s in sums]
    own = product(split(coef), (wt2h[...], wt2l[...]), dot)
    own = [own[:, 2 * RANK * k : 2 * RANK * (k + 1)] for k in range(2)]
    own[0] = own[0] + jnp.concatenate([half, coef], 1)
    receive = exchange(1, own)

    hpair[PAIR[4]] = gpair[PAIR[4]]

    for level in range(DEPTH - 2, -1, -1):

        def lower_two(m, level=level):
            parent = hpair[PAIR[level + 1] + m]
            for c in range(2):
                at = PAIR[level] + 2 * m + c
                w = (ltr_h[rows_at(at, 2 * RANK)], ltr_l[rows_at(at, 2 * RANK)])
                h = split(parent[:, RANK * c : RANK * (c + 1)])
                hpair[at] = gpair[at] + product(h, w, dot_t)

        sweep(LEAVES >> (level + 2), lower_two, 4)

    def far_leaf(p):
        h = hpair[p]
        h = jnp.concatenate([h[:, :RANK], h[:, RANK:]], 0)
        w = (bas_h[rows_at(p, 2 * LEAF)], bas_l[rows_at(p, 2 * LEAF)])
        far = product(split(h), w, dot_t)
        acc[:, rows_at(p, 2 * LEAF)] = jnp.where(low, far[:RHS], far[RHS:])

    sweep(LEAVES // 2, far_leaf, 4)

    for copy in halos:
        copy.wait()
    for target, edge in ((0, 0), (HALO + LEAVES, NODES - 1)):
        keep = jnp.where(me == edge, 0.0, 1.0)
        for j in range(target, target + HALO):
            blocks[j] = blocks[j] * keep

    def near_leaf(i):
        at = rows_at(i, LEAF)
        tx, ty, tz = (points[at, c : c + 1] for c in range(3))
        count = cnt_ref[i]
        kernels, charges = [], []
        for t in range(NNEAR // 2):
            j0 = off_ref[i, 2 * t] + (i + HALO)
            j1 = off_ref[i, 2 * t + 1] + (i + HALO)
            c = jnp.where(low, blocks[j0], blocks[j1 ^ 1])
            live = jnp.where(low, 2 * t, 2 * t + 1) < count
            charges.append(jnp.where(live, c[:RHS], 0.0))
            dx = tx - c[RHS : RHS + 1]
            dy = ty - c[RHS + 1 : RHS + 2]
            dz = tz - c[RHS + 2 : RHS + 3]
            kernels.append(lax.rsqrt(dx * dx + dy * dy + dz * dz + softening))
        return product(
            split(jnp.concatenate(charges, 1)), split(jnp.concatenate(kernels, 1)), dot_t
        )

    def near(p):
        tile = jnp.concatenate([near_leaf(2 * p), near_leaf(2 * p + 1)], 1)
        at = rows_at(p, 2 * LEAF)
        acc[:, at] = acc[:, at] + tile

    def near_some(first, last):
        lax.fori_loop(first, last, lambda p, carry: (near(p), carry)[1], 0)

    near_some(0, 4)

    sums = receive()
    tot = own[0] + (sums[0] + sums[1])
    coef = tot[:, :RANK]
    early += [s[:, RANK:] for s in sums]
    own = product(split(coef), (wt3h[...], wt3l[...]), dot)
    own = [jnp.concatenate([coef, half], 1), own[:, : 2 * RANK], own[:, 2 * RANK :]]
    receive = exchange(2, own)

    local = half
    for k in range(5):
        w = (wk_h[:, rows_at(k, RANK)], wk_l[:, rows_at(k, RANK)])
        local = local + product(split(early[k]), w, dot_t)

    top = rows_at(PAIR[4], 2 * RANK)
    gch[top] = ltr_h[top]
    gcl[top] = ltr_l[top]
    for level in range(DEPTH - 2, -1, -1):

        def compose(m, level=level):
            at = rows_at(PAIR[level] + m, 2 * RANK)
            up = rows_at(START[level + 1] + m, RANK)
            gch[at], gcl[at] = split(
                product((ltr_h[at], ltr_l[at]), (gch[up], gcl[up]), dot)
            )

        sweep(LEAVES >> (level + 1), compose, 4)

    def compose_leaf(i):
        at = rows_at(i, LEAF)
        dh[at], dl[at] = split(product((bas_h[at], bas_l[at]), (gch[at], gcl[at]), dot))

    sweep(LEAVES, compose_leaf, 4)
    near_some(4, 16)

    s5, s6, s7 = receive()
    tail = split(jnp.concatenate([s5 + s6, s7], 1))
    w = (wk_h[:, 5 * RANK :], wk_l[:, 5 * RANK :])
    local = split(local + product(tail, w, dot_t))
    for b in range(SPAN // 256):
        at = rows_at(b, 256)
        out_ref[:, at] = acc[:, at] + product(local, (dh[at], dl[at]), dot_t)


def per_device(
    densities, panels, areas, near_offsets, near_count,
    leaf_basis, local_trans, local_coupling, up_trans, coupling,
):
    hbm = pl.BlockSpec(memory_space=pltpu.HBM)
    smem = pl.BlockSpec(memory_space=pltpu.SMEM)
    nlocal = 2 * LEAVES - 2
    npeers = sum((1 << n) - 1 for _, n in PHASES)
    vm = pltpu.VMEM
    scratch = [
        vm((RHS, SPAN), f32),
        vm((3, SPAN), f32),
        vm((1, SPAN), f32),
        vm((LEAVES, LEAF, RANK), f32),
        vm((nlocal, RANK, RANK), f32),
        vm((nlocal, RANK, RANK), f32),
        vm((1, LEVELS, RANK, RANK), f32),
        vm((1, LEVELS, RANK, RANK), f32),
        vm((SPAN, RANK), bf16),
        vm((SPAN, RANK), bf16),
        vm((nlocal * RANK, RANK), bf16),
        vm((nlocal * RANK, RANK), bf16),
        vm((nlocal * RANK, RANK), bf16),
        vm((nlocal * RANK, RANK), bf16),
        vm((SPAN, RANK), bf16),
        vm((SPAN, RANK), bf16),
        vm((LEAVES + 2 * HALO, 24, 2 * LEAF), f32),
        vm((SPAN, 8), f32),
        vm((nlocal // 2, 2 * RHS, RANK), f32),
        vm((nlocal // 2, RHS, 2 * RANK), f32),
        vm((nlocal // 2, RHS, 2 * RANK), f32),
        vm((RHS, SPAN), f32),
        vm((RANK, 6 * RANK), bf16),
        vm((RANK, 6 * RANK), bf16),
        vm((RANK, 4 * RANK), bf16),
        vm((RANK, 4 * RANK), bf16),
        vm((RANK, 4 * RANK), bf16),
        vm((RANK, 4 * RANK), bf16),
        vm((RANK, 9 * RANK), bf16),
        vm((RANK, 9 * RANK), bf16),
        vm((LEVELS, RHS, 2 * RANK), f32),
        vm((npeers, RHS, 2 * RANK), f32),
        pltpu.SemaphoreType.DMA((8,)),
        pltpu.SemaphoreType.DMA((npeers,)),
        pltpu.SemaphoreType.DMA((npeers,)),
        pltpu.SemaphoreType.DMA((2,)),
        pltpu.SemaphoreType.DMA((2,)),
    ]
    return pl.pallas_call(
        kernel,
        out_shape=jax.ShapeDtypeStruct((RHS, SPAN), f32),
        in_specs=[hbm, hbm, hbm, smem, smem, hbm, hbm, hbm, hbm, hbm],
        out_specs=pl.BlockSpec(memory_space=pltpu.VMEM),
        scratch_shapes=scratch,
        compiler_params=pltpu.CompilerParams(
            collective_id=0, has_side_effects=True, vmem_limit_bytes=40 * 1024 * 1024
        ),
    )(
        densities, panels, areas.reshape(1, SPAN), near_offsets, near_count,
        leaf_basis, local_trans, local_coupling, up_trans, coupling,
    )


def solution(mesh):
    return jax.shard_map(
        per_device,
        mesh=mesh,
        in_specs=(
            P(None, "leaf"),
            P(None, "leaf"),
            P("leaf"),
            P("leaf", None),
            P("leaf"),
            P("leaf", None, None),
            P("leaf", None, None),
            P("leaf", None, None),
            P("leaf", None, None, None),
            P("leaf", None, None, None),
        ),
        out_specs=P(None, "leaf"),
        check_vma=False,
    )
```

```python
import jax
import jax.numpy as jnp
from jax import lax
from jax.experimental import pallas as pl
from jax.experimental.pallas import tpu as pltpu
from jax.sharding import PartitionSpec as P

LEAF = 64
RANK = 64
RHS = 16
LEAVES = 32
HALO = 4
NNEAR = 6
LEVELS = 8
DEPTH = 5
NODES = 256
SPAN = LEAVES * LEAF
softening = 0.25
MESH = pl.DeviceIdType.MESH
f32 = jnp.float32
bf16 = jnp.bfloat16

PHASES = ((0, 3), (3, 2), (5, 3))
START = [2 * LEAVES - 2 * (LEAVES >> j) for j in range(DEPTH)]
PAIR = [s // 2 for s in START]


def split(x):
    high = x.astype(bf16)
    return high, (x - high.astype(f32)).astype(bf16)


def dot(a, b):
    return lax.dot_general(a, b, (((1,), (0,)), ((), ())), preferred_element_type=f32)


def dot_t(a, b):
    return lax.dot_general(a, b, (((1,), (1,)), ((), ())), preferred_element_type=f32)


def product(a, b, op):
    ah, al = a
    bh, bl = b
    rows = ah.shape[0]
    both = op(jnp.concatenate([ah, al], 0), bh)
    return both[:rows] + (both[rows:] + op(ah, bl))


def sweep(count, body, unroll):
    if count <= unroll:
        for i in range(count):
            body(i)
        return

    def step(i, carry):
        for u in range(unroll):
            body(i * unroll + u)
        return carry

    lax.fori_loop(0, count // unroll, step, 0)


def rows_at(index, count):
    if isinstance(index, int):
        return slice(index * count, (index + 1) * count)
    return pl.ds(pl.multiple_of(index * count, count), count)


def kernel(
    dens_hbm, pan_hbm, area_hbm, off_hbm, cnt_hbm, bas_hbm, ltr_hbm, lco_hbm, upt_hbm, cpl_hbm,
    out_hbm,
    out_ref, off_ref, cnt_ref, dens, pan, area, bas, ltr, lco, upt, cpl,
    bas_h, bas_l, ltr_h, ltr_l, gch, gcl, dh, dl,
    blocks, points, qrow, gpair, hpair, acc,
    wt1h, wt1l, wt2h, wt2l, wt3h, wt3l, wk_h, wk_l,
    send, recv, load_sem, store_sem, send_sem, recv_sem, halo_ssem, halo_rsem,
):
    me = lax.axis_index("leaf")
    right = lax.rem(me + 1, NODES)
    left = lax.rem(me + NODES - 1, NODES)
    loads = {}
    for at, (name, src, dst) in enumerate(
        (
            ("dens", dens_hbm, dens),
            ("bas", bas_hbm, bas),
            ("ltr", ltr_hbm, ltr),
            ("upt", upt_hbm, upt),
            ("pan", pan_hbm, pan),
            ("area", area_hbm, area),
            ("off", off_hbm, off_ref),
            ("cnt", cnt_hbm, cnt_ref),
            ("lco", lco_hbm, lco),
            ("cpl", cpl_hbm, cpl),
        )
    ):
        loads[name] = pltpu.make_async_copy(src, dst, load_sem.at[at])
        loads[name].start()

    barrier = pltpu.get_barrier_semaphore()
    peers = [p << first for first, levels in PHASES for p in range(1, 1 << levels)]
    for p in peers:
        pl.semaphore_signal(barrier, inc=1, device_id=(me ^ p,), device_id_type=MESH)
    for neighbour in (left, right):
        pl.semaphore_signal(barrier, inc=1, device_id=(neighbour,), device_id_type=MESH)

    lane = lax.broadcasted_iota(jnp.int32, (1, 2 * LEAF), 1)
    low = lane < LEAF
    half = jnp.zeros((RHS, LEAF), f32)

    loads["dens"].wait()
    loads["bas"].wait()

    def moments(p):
        x = dens[:, rows_at(p, 2 * LEAF)]
        x = jnp.concatenate([jnp.where(low, x, 0.0), jnp.where(low, 0.0, x)], 0)
        w = split(bas[rows_at(p, 2)].reshape(2 * LEAF, RANK))
        bas_h[rows_at(p, 2 * LEAF)] = w[0]
        bas_l[rows_at(p, 2 * LEAF)] = w[1]
        qrow[p] = product(split(x), w, dot)

    sweep(LEAVES // 2, moments, 16)
    loads["ltr"].wait()

    def lift(level, p):
        q = qrow[PAIR[level] + p]
        q = jnp.concatenate([q[:RHS], q[RHS:]], 1)
        at = PAIR[level] + p
        w = split(ltr[rows_at(at, 2)].reshape(2 * RANK, RANK))
        ltr_h[rows_at(at, 2 * RANK)] = w[0]
        ltr_l[rows_at(at, 2 * RANK)] = w[1]
        return product(split(q), w, dot)

    for level in range(DEPTH - 1):

        def lift_two(m, level=level):
            qrow[PAIR[level + 1] + m] = jnp.concatenate(
                [lift(level, 2 * m), lift(level, 2 * m + 1)], 0
            )

        sweep(LEAVES >> (level + 2), lift_two, 16)
    loads["upt"].wait()

    e = [split(upt[0, k]) for k in range(LEVELS - 1)]
    zero = jnp.zeros((RANK, RANK), f32)

    def chain(first, count):
        out = [upt[0, first]]
        for k in range(first + 1, first + count):
            out.append(product(split(out[-1]), e[k], dot))
        return out

    t1, t2, t3 = chain(0, 3)
    wt1h[...], wt1l[...] = split(jnp.concatenate([t3, zero, t3, t1, t3, t2], 1))
    coef = lift(DEPTH - 1, 0)

    def exchange(phase, messages):
        first, levels = PHASES[phase]
        base = sum((1 << n) - 1 for _, n in PHASES[:phase])
        slot = sum(n for _, n in PHASES[:phase])
        for k in range(levels):
            send[slot + k] = messages[k]
        copies = []
        for p in reversed(range(1, 1 << levels)):
            copy = pltpu.make_async_remote_copy(
                src_ref=send.at[slot + p.bit_length() - 1],
                dst_ref=recv.at[base + p - 1],
                send_sem=send_sem.at[base + p - 1],
                recv_sem=recv_sem.at[base + p - 1],
                device_id=(me ^ (p << first),),
                device_id_type=MESH,
            )
            copy.start()
            copies.append(copy)

        def receive():
            for copy in copies:
                copy.wait()
            sums = []
            for k in range(levels):
                parts = [recv[base + p - 1] for p in range(1 << k, 2 << k)]
                while len(parts) > 1:
                    parts = [a + b for a, b in zip(parts[::2], parts[1::2])]
                sums.append(parts[0])
            return sums

        return receive

    own = product(split(coef), (wt1h[...], wt1l[...]), dot)
    own = [own[:, 2 * RANK * k : 2 * RANK * (k + 1)] for k in range(3)]
    own[0] = own[0] + jnp.concatenate([half, coef], 1)
    pl.semaphore_wait(barrier, len(peers) + 2)
    receive = exchange(0, own)

    loads["pan"].wait()
    loads["area"].wait()
    halo_rows = jnp.zeros((5, 2 * LEAF), f32)

    def pack(p):
        at = rows_at(p, 2 * LEAF)
        coords = jnp.concatenate([pan[:, at], halo_rows], 0)
        tile = jnp.concatenate([dens[:, at] * area[:, at], coords], 0)
        blocks[HALO + 2 * p] = tile
        blocks[HALO + 2 * p + 1] = pltpu.roll(tile, LEAF, 1)
        points[at, :] = coords.T

    sweep(LEAVES // 2, pack, 16)
    halos = []
    for at, (source, target, device) in enumerate(
        ((LEAVES, 0, right), (HALO, HALO + LEAVES, left))
    ):
        copy = pltpu.make_async_remote_copy(
            src_ref=blocks.at[pl.ds(source, HALO)],
            dst_ref=blocks.at[pl.ds(target, HALO)],
            send_sem=halo_ssem.at[at],
            recv_sem=halo_rsem.at[at],
            device_id=(device,),
            device_id_type=MESH,
        )
        copy.start()
        halos.append(copy)

    u4, u5 = chain(3, 2)
    wt2h[...], wt2l[...] = split(jnp.concatenate([u5, zero, u5, u4], 1))
    v6, v7 = chain(5, 2)
    wt3h[...], wt3l[...] = split(jnp.concatenate([zero, v6, v7, zero], 1))
    loads["cpl"].wait()
    t4 = product(split(t3), e[3], dot)
    t5 = product(split(t3), split(u5), dot)
    t6 = product(split(t5), e[5], dot)
    t7 = product(split(t5), split(v7), dot)
    blank = jnp.zeros((RANK, RANK), bf16)
    wk_h[:, rows_at(LEVELS, RANK)] = blank
    wk_l[:, rows_at(LEVELS, RANK)] = blank
    for k, t in enumerate((None, t1, t2, t3, t4, t5, t6, t7)):
        w = cpl[0, k] if t is None else product(split(t), split(cpl[0, k]), dot)
        wk_h[:, rows_at(k, RANK)], wk_l[:, rows_at(k, RANK)] = split(w)

    loads["lco"].wait()

    def couple(p):
        q = qrow[p]
        q = jnp.concatenate([q[RHS:], q[:RHS]], 0)
        w = split(lco[rows_at(p, 2)].reshape(2 * RANK, RANK))
        g = product(split(q), w, dot_t)
        gpair[p] = jnp.where(low, g[:RHS], g[RHS:])

    sweep(28, couple, 14)
    for p in range(28, 31):
        couple(p)

    sums = receive()
    tot = own[0] + (sums[0] + (sums[1] + sums[2]))
    coef = tot[:, :RANK]
    early = [s[:, RANK:] for s in sums]
    own = product(split(coef), (wt2h[...], wt2l[...]), dot)
    own = [own[:, 2 * RANK * k : 2 * RANK * (k + 1)] for k in range(2)]
    own[0] = own[0] + jnp.concatenate([half, coef], 1)
    receive = exchange(1, own)

    hpair[PAIR[4]] = gpair[PAIR[4]]

    for level in range(DEPTH - 2, -1, -1):

        def lower_two(m, level=level):
            parent = hpair[PAIR[level + 1] + m]
            for c in range(2):
                at = PAIR[level] + 2 * m + c
                w = (ltr_h[rows_at(at, 2 * RANK)], ltr_l[rows_at(at, 2 * RANK)])
                h = split(parent[:, RANK * c : RANK * (c + 1)])
                hpair[at] = gpair[at] + product(h, w, dot_t)

        sweep(LEAVES >> (level + 2), lower_two, 16)

    def far_leaf(p):
        h = hpair[p]
        h = jnp.concatenate([h[:, :RANK], h[:, RANK:]], 0)
        w = (bas_h[rows_at(p, 2 * LEAF)], bas_l[rows_at(p, 2 * LEAF)])
        far = product(split(h), w, dot_t)
        acc[:, rows_at(p, 2 * LEAF)] = jnp.where(low, far[:RHS], far[RHS:])

    sweep(LEAVES // 2, far_leaf, 16)

    loads["off"].wait()
    loads["cnt"].wait()
    for copy in halos:
        copy.wait()
    for target, edge in ((0, 0), (HALO + LEAVES, NODES - 1)):
        keep = jnp.where(me == edge, 0.0, 1.0)
        for j in range(target, target + HALO):
            blocks[j] = blocks[j] * keep

    def near_leaf(i):
        at = rows_at(i, LEAF)
        tx, ty, tz = (points[at, c : c + 1] for c in range(3))
        count = cnt_ref[i]
        kernels, charges = [], []
        for t in range(NNEAR // 2):
            j0 = off_ref[2 * t, i] + (i + HALO)
            j1 = off_ref[2 * t + 1, i] + (i + HALO)
            c = jnp.where(low, blocks[j0], blocks[j1 ^ 1])
            live = jnp.where(low, 2 * t, 2 * t + 1) < count
            charges.append(jnp.where(live, c[:RHS], 0.0))
            dx = tx - c[RHS : RHS + 1]
            dy = ty - c[RHS + 1 : RHS + 2]
            dz = tz - c[RHS + 2 : RHS + 3]
            kernels.append(lax.rsqrt(dx * dx + dy * dy + dz * dz + softening))
        return product(
            split(jnp.concatenate(charges, 1)), split(jnp.concatenate(kernels, 1)), dot_t
        )

    def near(p):
        tile = jnp.concatenate([near_leaf(2 * p), near_leaf(2 * p + 1)], 1)
        at = rows_at(p, 2 * LEAF)
        acc[:, at] = acc[:, at] + tile

    def near_some(first, last):
        lax.fori_loop(first // 2, last // 2, lambda p, carry: (near(2 * p), near(2 * p + 1), carry)[2], 0)

    near_some(0, 8)

    sums = receive()
    tot = own[0] + (sums[0] + sums[1])
    coef = tot[:, :RANK]
    early += [s[:, RANK:] for s in sums]
    own = product(split(coef), (wt3h[...], wt3l[...]), dot)
    own = [jnp.concatenate([coef, half], 1), own[:, : 2 * RANK], own[:, 2 * RANK :]]
    receive = exchange(2, own)

    local = half
    for k in range(5):
        w = (wk_h[:, rows_at(k, RANK)], wk_l[:, rows_at(k, RANK)])
        local = local + product(split(early[k]), w, dot_t)

    top = rows_at(PAIR[4], 2 * RANK)
    gch[top] = ltr_h[top]
    gcl[top] = ltr_l[top]
    for level in range(DEPTH - 2, -1, -1):

        def compose(m, level=level):
            at = rows_at(PAIR[level] + m, 2 * RANK)
            up = rows_at(START[level + 1] + m, RANK)
            gch[at], gcl[at] = split(
                product((ltr_h[at], ltr_l[at]), (gch[up], gcl[up]), dot)
            )

        sweep(LEAVES >> (level + 1), compose, 16)

    def compose_leaf(i):
        at = rows_at(i, LEAF)
        dh[at], dl[at] = split(product((bas_h[at], bas_l[at]), (gch[at], gcl[at]), dot))

    sweep(LEAVES, compose_leaf, 16)
    near_some(8, 16)

    s5, s6, s7 = receive()
    tail = split(jnp.concatenate([s5 + s6, s7], 1))
    w = (wk_h[:, 5 * RANK :], wk_l[:, 5 * RANK :])
    local = split(local + product(tail, w, dot_t))
    stores = []
    for b in range(4):
        at = rows_at(b, 512)
        out_ref[:, at] = acc[:, at] + product(local, (dh[at], dl[at]), dot_t)
        stores.append(pltpu.make_async_copy(out_ref.at[:, at], out_hbm.at[:, at], store_sem.at[b]))
        stores[-1].start()
    for copy in stores:
        copy.wait()


def per_device(
    densities, panels, areas, near_offsets, near_count,
    leaf_basis, local_trans, local_coupling, up_trans, coupling,
):
    hbm = pl.BlockSpec(memory_space=pltpu.HBM)
    nlocal = 2 * LEAVES - 2
    npeers = sum((1 << n) - 1 for _, n in PHASES)
    vm = pltpu.VMEM
    scratch = [
        vm((RHS, SPAN), f32),
        pltpu.SMEM((NNEAR, LEAVES), jnp.int32),
        pltpu.SMEM((LEAVES,), jnp.int32),
        vm((RHS, SPAN), f32),
        vm((3, SPAN), f32),
        vm((1, SPAN), f32),
        vm((LEAVES, LEAF, RANK), f32),
        vm((nlocal, RANK, RANK), f32),
        vm((nlocal, RANK, RANK), f32),
        vm((1, LEVELS, RANK, RANK), f32),
        vm((1, LEVELS, RANK, RANK), f32),
        vm((SPAN, RANK), bf16),
        vm((SPAN, RANK), bf16),
        vm((nlocal * RANK, RANK), bf16),
        vm((nlocal * RANK, RANK), bf16),
        vm((nlocal * RANK, RANK), bf16),
        vm((nlocal * RANK, RANK), bf16),
        vm((SPAN, RANK), bf16),
        vm((SPAN, RANK), bf16),
        vm((LEAVES + 2 * HALO, 24, 2 * LEAF), f32),
        vm((SPAN, 8), f32),
        vm((nlocal // 2, 2 * RHS, RANK), f32),
        vm((nlocal // 2, RHS, 2 * RANK), f32),
        vm((nlocal // 2, RHS, 2 * RANK), f32),
        vm((RHS, SPAN), f32),
        vm((RANK, 6 * RANK), bf16),
        vm((RANK, 6 * RANK), bf16),
        vm((RANK, 4 * RANK), bf16),
        vm((RANK, 4 * RANK), bf16),
        vm((RANK, 4 * RANK), bf16),
        vm((RANK, 4 * RANK), bf16),
        vm((RANK, 9 * RANK), bf16),
        vm((RANK, 9 * RANK), bf16),
        vm((LEVELS, RHS, 2 * RANK), f32),
        vm((npeers, RHS, 2 * RANK), f32),
        pltpu.SemaphoreType.DMA((10,)),
        pltpu.SemaphoreType.DMA((4,)),
        pltpu.SemaphoreType.DMA((npeers,)),
        pltpu.SemaphoreType.DMA((npeers,)),
        pltpu.SemaphoreType.DMA((2,)),
        pltpu.SemaphoreType.DMA((2,)),
    ]
    return pl.pallas_call(
        kernel,
        out_shape=jax.ShapeDtypeStruct((RHS, SPAN), f32),
        in_specs=[hbm] * 10,
        out_specs=hbm,
        scratch_shapes=scratch,
        compiler_params=pltpu.CompilerParams(
            collective_id=0, has_side_effects=True, vmem_limit_bytes=63 * 1024 * 1024
        ),
    )(
        densities, panels, areas.reshape(1, SPAN), near_offsets.T, near_count,
        leaf_basis, local_trans, local_coupling, up_trans, coupling,
    )


def solution(mesh):
    return jax.shard_map(
        per_device,
        mesh=mesh,
        in_specs=(
            P(None, "leaf"),
            P(None, "leaf"),
            P("leaf"),
            P("leaf", None),
            P("leaf"),
            P("leaf", None, None),
            P("leaf", None, None),
            P("leaf", None, None),
            P("leaf", None, None, None),
            P("leaf", None, None, None),
        ),
        out_specs=P(None, "leaf"),
        check_vma=False,
    )
```

```python
import jax
import jax.numpy as jnp
from jax import lax
from jax.experimental import pallas as pl
from jax.experimental.pallas import tpu as pltpu
from jax.sharding import PartitionSpec as P

LEAF = 64
RANK = 64
RHS = 16
LEAVES = 32
HALO = 4
NNEAR = 6
LEVELS = 8
DEPTH = 5
NODES = 256
SPAN = LEAVES * LEAF
NOLEAF = LEAVES + 2 * HALO
softening = 0.25
MESH = pl.DeviceIdType.MESH
f32 = jnp.float32
bf16 = jnp.bfloat16

PHASES = ((0, 3), (3, 2), (5, 3))
START = [2 * LEAVES - 2 * (LEAVES >> j) for j in range(DEPTH)]
PAIR = [s // 2 for s in START]


def hops(p):
    count = 0
    for bits, size in ((p >> 1 & 3, 4), (p >> 3 & 3, 4), (p >> 5, 8)):
        count += max(min((a ^ bits) - a & size - 1, a - (a ^ bits) & size - 1) for a in range(size))
    return count


def split(x):
    high = x.astype(bf16)
    return high, (x - high.astype(f32)).astype(bf16)


def dot(a, b):
    return lax.dot_general(a, b, (((1,), (0,)), ((), ())), preferred_element_type=f32)


def dot_t(a, b):
    return lax.dot_general(a, b, (((1,), (1,)), ((), ())), preferred_element_type=f32)


def product(a, b, op):
    ah, al = a
    bh, bl = b
    rows = ah.shape[0]
    both = op(jnp.concatenate([ah, al], 0), bh)
    return both[:rows] + (both[rows:] + op(ah, bl))


def sweep(count, body, unroll):
    if count <= unroll:
        for i in range(count):
            body(i)
        return

    def step(i, carry):
        for u in range(unroll):
            body(i * unroll + u)
        return carry

    lax.fori_loop(0, count // unroll, step, 0)


def rows_at(index, count):
    if isinstance(index, int):
        return slice(index * count, (index + 1) * count)
    return pl.ds(pl.multiple_of(index * count, count), count)


def kernel(
    dens_hbm, pan_hbm, area_hbm, off_hbm, cnt_hbm, bas_hbm, ltr_hbm, lco_hbm, upt_hbm, cpl_hbm,
    out_ref,
    off_ref, cnt_ref, dens, pan, area, bas, ltr, lco, upt, cpl,
    bas_h, bas_l, ltr_h, ltr_l, gch, gcl, dh, dl,
    coords, charge, ends, halo, column, points, qrow, gpair, hpair, acc,
    wt1h, wt1l, wt2h, wt2l, wt3h, wt3l, wk_h, wk_l,
    send, recv, load_sem, send_sem, recv_sem, halo_ssem, halo_rsem,
):
    me = lax.axis_index("leaf")
    right = lax.rem(me + 1, NODES)
    left = lax.rem(me + NODES - 1, NODES)
    loads = {}
    for at, (name, src, dst) in enumerate(
        (
            ("dens", dens_hbm, dens),
            ("bas", bas_hbm, bas),
            ("ltr", ltr_hbm, ltr),
            ("upt", upt_hbm, upt),
            ("pan", pan_hbm, pan),
            ("area", area_hbm, area),
            ("off", off_hbm, off_ref),
            ("cnt", cnt_hbm, cnt_ref),
            ("lco", lco_hbm, lco),
            ("cpl", cpl_hbm, cpl),
        )
    ):
        loads[name] = pltpu.make_async_copy(src, dst, load_sem.at[at])
        loads[name].start()

    barrier = pltpu.get_barrier_semaphore()
    peers = [p << first for first, levels in PHASES for p in range(1, 1 << levels)]
    for p in peers:
        pl.semaphore_signal(barrier, inc=1, device_id=(me ^ p,), device_id_type=MESH)
    for neighbour in (left, right):
        pl.semaphore_signal(barrier, inc=1, device_id=(neighbour,), device_id_type=MESH)

    lane = lax.broadcasted_iota(jnp.int32, (1, 2 * LEAF), 1)
    low = lane < LEAF
    half = jnp.zeros((RHS, LEAF), f32)

    loads["dens"].wait()
    loads["bas"].wait()

    def moments(p):
        x = dens[:, rows_at(p, 2 * LEAF)]
        x = jnp.concatenate([jnp.where(low, x, 0.0), jnp.where(low, 0.0, x)], 0)
        w = split(bas[rows_at(p, 2)].reshape(2 * LEAF, RANK))
        bas_h[rows_at(p, 2 * LEAF)] = w[0]
        bas_l[rows_at(p, 2 * LEAF)] = w[1]
        qrow[p] = product(split(x), w, dot)

    sweep(LEAVES // 2, moments, 16)
    loads["ltr"].wait()

    def lift(level, p):
        q = qrow[PAIR[level] + p]
        q = jnp.concatenate([q[:RHS], q[RHS:]], 1)
        at = PAIR[level] + p
        w = split(ltr[rows_at(at, 2)].reshape(2 * RANK, RANK))
        ltr_h[rows_at(at, 2 * RANK)] = w[0]
        ltr_l[rows_at(at, 2 * RANK)] = w[1]
        return product(split(q), w, dot)

    for level in range(DEPTH - 1):

        def lift_two(m, level=level):
            qrow[PAIR[level + 1] + m] = jnp.concatenate(
                [lift(level, 2 * m), lift(level, 2 * m + 1)], 0
            )

        sweep(LEAVES >> (level + 2), lift_two, 16)
    loads["upt"].wait()

    e = [split(upt[0, k]) for k in range(LEVELS - 1)]
    zero = jnp.zeros((RANK, RANK), f32)

    def chain(first, count):
        out = [upt[0, first]]
        for k in range(first + 1, first + count):
            out.append(product(split(out[-1]), e[k], dot))
        return out

    t1, t2, t3 = chain(0, 3)
    wt1h[...], wt1l[...] = split(jnp.concatenate([t3, zero, t3, t1, t3, t2], 1))
    coef = lift(DEPTH - 1, 0)

    def exchange(phase, messages):
        first, levels = PHASES[phase]
        base = sum((1 << n) - 1 for _, n in PHASES[:phase])
        slot = sum(n for _, n in PHASES[:phase])
        for k in range(levels):
            send[slot + k] = messages[k]
        copies = []
        for p in sorted(range(1, 1 << levels), key=lambda p: -hops(p << first)):
            copy = pltpu.make_async_remote_copy(
                src_ref=send.at[slot + p.bit_length() - 1],
                dst_ref=recv.at[base + p - 1],
                send_sem=send_sem.at[base + p - 1],
                recv_sem=recv_sem.at[base + p - 1],
                device_id=(me ^ (p << first),),
                device_id_type=MESH,
            )
            copy.start()
            copies.append(copy)

        def receive():
            for copy in copies:
                copy.wait()
            sums = []
            for k in range(levels):
                parts = [recv[base + p - 1] for p in range(1 << k, 2 << k)]
                while len(parts) > 1:
                    parts = [a + b for a, b in zip(parts[::2], parts[1::2])]
                sums.append(parts[0])
            return sums

        return receive

    own = product(split(coef), (wt1h[...], wt1l[...]), dot)
    own = [own[:, 2 * RANK * k : 2 * RANK * (k + 1)] for k in range(3)]
    own[0] = own[0] + jnp.concatenate([half, coef], 1)
    pl.semaphore_wait(barrier, len(peers) + 2)
    receive = exchange(0, own)

    loads["pan"].wait()
    loads["area"].wait()
    halo_rows = jnp.zeros((5, 2 * LEAF), f32)

    def place(tile, slot):
        coords[slot] = tile[RHS:]
        coords[slot + 1] = pltpu.roll(tile[RHS:], LEAF, 1)
        high, rest = split(tile[:RHS].T)
        charge[pl.ds(slot, 2)] = jnp.concatenate([high, rest], 1).reshape(2, LEAF, 2 * RHS)

    def pack(p):
        at = rows_at(p, 2 * LEAF)
        where = jnp.concatenate([pan[:, at], halo_rows], 0)
        tile = jnp.concatenate([dens[:, at] * area[:, at], where], 0)
        if p in (0, 1, 14, 15):
            ends[p if p < 2 else p - 12] = tile
        place(tile, HALO + 2 * p)
        points[at, :] = where.T

    for p in (0, 1, 14, 15):
        pack(p)
    halos = []
    for at, (source, target, device) in enumerate(((2, 0, right), (0, 2, left))):
        copy = pltpu.make_async_remote_copy(
            src_ref=ends.at[pl.ds(source, 2)],
            dst_ref=halo.at[pl.ds(target, 2)],
            send_sem=halo_ssem.at[at],
            recv_sem=halo_rsem.at[at],
            device_id=(device,),
            device_id_type=MESH,
        )
        copy.start()
        halos.append(copy)
    for p in range(2, 14):
        pack(p)
    coords[NOLEAF] = jnp.zeros((8, 2 * LEAF), f32)
    coords[NOLEAF + 1] = jnp.zeros((8, 2 * LEAF), f32)
    charge[NOLEAF] = jnp.zeros((LEAF, 2 * RHS), bf16)

    u4, u5 = chain(3, 2)
    wt2h[...], wt2l[...] = split(jnp.concatenate([u5, zero, u5, u4], 1))
    v6, v7 = chain(5, 2)
    wt3h[...], wt3l[...] = split(jnp.concatenate([zero, v6, v7, zero], 1))
    loads["cpl"].wait()
    t4 = product(split(t3), e[3], dot)
    t5 = product(split(t3), split(u5), dot)
    t6 = product(split(t5), e[5], dot)
    t7 = product(split(t5), split(v7), dot)
    blank = jnp.zeros((RANK, RANK), bf16)
    wk_h[:, rows_at(LEVELS, RANK)] = blank
    wk_l[:, rows_at(LEVELS, RANK)] = blank
    for k, t in enumerate((None, t1, t2, t3, t4, t5, t6, t7)):
        w = cpl[0, k] if t is None else product(split(t), split(cpl[0, k]), dot)
        wk_h[:, rows_at(k, RANK)], wk_l[:, rows_at(k, RANK)] = split(w)

    loads["lco"].wait()

    def couple(p):
        q = qrow[p]
        q = jnp.concatenate([q[RHS:], q[:RHS]], 0)
        w = split(lco[rows_at(p, 2)].reshape(2 * RANK, RANK))
        g = product(split(q), w, dot_t)
        gpair[p] = jnp.where(low, g[:RHS], g[RHS:])

    sweep(28, couple, 14)
    for p in range(28, 31):
        couple(p)

    sums = receive()
    tot = own[0] + (sums[0] + (sums[1] + sums[2]))
    coef = tot[:, :RANK]
    early = [s[:, RANK:] for s in sums]
    own = product(split(coef), (wt2h[...], wt2l[...]), dot)
    own = [own[:, 2 * RANK * k : 2 * RANK * (k + 1)] for k in range(2)]
    own[0] = own[0] + jnp.concatenate([half, coef], 1)
    receive = exchange(1, own)

    hpair[PAIR[4]] = gpair[PAIR[4]]

    for level in range(DEPTH - 2, -1, -1):

        def lower_two(m, level=level):
            parent = hpair[PAIR[level + 1] + m]
            for c in range(2):
                at = PAIR[level] + 2 * m + c
                w = (ltr_h[rows_at(at, 2 * RANK)], ltr_l[rows_at(at, 2 * RANK)])
                h = split(parent[:, RANK * c : RANK * (c + 1)])
                hpair[at] = gpair[at] + product(h, w, dot_t)

        sweep(LEAVES >> (level + 2), lower_two, 16)

    def far_leaf(p):
        h = hpair[p]
        h = jnp.concatenate([h[:, :RANK], h[:, RANK:]], 0)
        w = (bas_h[rows_at(p, 2 * LEAF)], bas_l[rows_at(p, 2 * LEAF)])
        far = product(split(h), w, dot_t)
        acc[:, rows_at(p, 2 * LEAF)] = jnp.where(low, far[:RHS], far[RHS:])

    sweep(LEAVES // 2, far_leaf, 16)

    loads["off"].wait()
    loads["cnt"].wait()
    for copy in halos:
        copy.wait()
    for end, slot, edge in ((0, 0, 0), (2, HALO + LEAVES, NODES - 1)):
        keep = jnp.where(me == edge, 0.0, 1.0)
        for t in range(2):
            place(halo[end + t] * keep, slot + 2 * t)

    def near_leaf(i):
        at = rows_at(i, LEAF)
        tx, ty, tz = (jnp.broadcast_to(points[at, c : c + 1], (LEAF, 2 * LEAF)) for c in range(3))
        count = cnt_ref[i]
        kernels, charges = [], []
        for t in range(NNEAR // 2):
            j = [
                jnp.where(s < count, off_ref[s, i] + (i + HALO), NOLEAF)
                for s in (2 * t, 2 * t + 1)
            ]
            charges += [charge[j[0]], charge[j[1]]]
            c = jnp.where(low, coords[j[0]], coords[j[1] ^ 1])
            dx = tx - c[0:1]
            dy = ty - c[1:2]
            dz = tz - c[2:3]
            kernels.append(lax.rsqrt(dx * dx + dy * dy + (dz * dz + softening)))
        high, rest = split(jnp.concatenate(kernels, 1))
        both = dot(jnp.concatenate([high, rest], 0), jnp.concatenate(charges, 0))
        column[at, :] = both[:LEAF] + both[LEAF:]

    def near(p):
        near_leaf(2 * p)
        near_leaf(2 * p + 1)

    def near_fold(p):
        at = rows_at(p, 2 * LEAF)
        tile = column[at, :].T
        acc[:, at] = acc[:, at] + (tile[:RHS] + tile[RHS:])

    def near_some(first, last):
        sweep(last - first, lambda p: near(p + first), 4)

    near_some(0, 8)

    sums = receive()
    tot = own[0] + (sums[0] + sums[1])
    coef = tot[:, :RANK]
    early += [s[:, RANK:] for s in sums]
    own = product(split(coef), (wt3h[...], wt3l[...]), dot)
    own = [jnp.concatenate([coef, half], 1), own[:, : 2 * RANK], own[:, 2 * RANK :]]
    receive = exchange(2, own)

    local = half
    for k in range(5):
        w = (wk_h[:, rows_at(k, RANK)], wk_l[:, rows_at(k, RANK)])
        local = local + product(split(early[k]), w, dot_t)

    top = rows_at(PAIR[4], 2 * RANK)
    gch[top] = ltr_h[top]
    gcl[top] = ltr_l[top]
    for level in range(DEPTH - 2, -1, -1):

        def compose(m, level=level):
            at = rows_at(PAIR[level] + m, 2 * RANK)
            up = rows_at(START[level + 1] + m, RANK)
            gch[at], gcl[at] = split(
                product((ltr_h[at], ltr_l[at]), (gch[up], gcl[up]), dot)
            )

        sweep(LEAVES >> (level + 1), compose, 16)

    def compose_leaf(i):
        at = rows_at(i, LEAF)
        dh[at], dl[at] = split(product((bas_h[at], bas_l[at]), (gch[at], gcl[at]), dot))

    sweep(LEAVES, compose_leaf, 16)
    near_some(8, 16)
    for p in range(LEAVES // 2):
        near_fold(p)

    s5, s6, s7 = receive()
    tail = split(jnp.concatenate([s5 + s6, s7], 1))
    w = (wk_h[:, 5 * RANK :], wk_l[:, 5 * RANK :])
    local = split(local + product(tail, w, dot_t))
    for b in range(4):
        at = rows_at(b, 512)
        out_ref[:, at] = acc[:, at] + product(local, (dh[at], dl[at]), dot_t)


def per_device(
    densities, panels, areas, near_offsets, near_count,
    leaf_basis, local_trans, local_coupling, up_trans, coupling,
):
    hbm = pl.BlockSpec(memory_space=pltpu.HBM)
    nlocal = 2 * LEAVES - 2
    npeers = sum((1 << n) - 1 for _, n in PHASES)
    vm = pltpu.VMEM
    scratch = [
        pltpu.SMEM((NNEAR, LEAVES), jnp.int32),
        pltpu.SMEM((LEAVES,), jnp.int32),
        vm((RHS, SPAN), f32),
        vm((3, SPAN), f32),
        vm((1, SPAN), f32),
        vm((LEAVES, LEAF, RANK), f32),
        vm((nlocal, RANK, RANK), f32),
        vm((nlocal, RANK, RANK), f32),
        vm((1, LEVELS, RANK, RANK), f32),
        vm((1, LEVELS, RANK, RANK), f32),
        vm((SPAN, RANK), bf16),
        vm((SPAN, RANK), bf16),
        vm((nlocal * RANK, RANK), bf16),
        vm((nlocal * RANK, RANK), bf16),
        vm((nlocal * RANK, RANK), bf16),
        vm((nlocal * RANK, RANK), bf16),
        vm((SPAN, RANK), bf16),
        vm((SPAN, RANK), bf16),
        vm((NOLEAF + 2, 8, 2 * LEAF), f32),
        vm((NOLEAF + 1, LEAF, 2 * RHS), bf16),
        vm((4, RHS + 8, 2 * LEAF), f32),
        vm((4, RHS + 8, 2 * LEAF), f32),
        vm((SPAN, 2 * RHS), f32),
        vm((SPAN, 8), f32),
        vm((nlocal // 2, 2 * RHS, RANK), f32),
        vm((nlocal // 2, RHS, 2 * RANK), f32),
        vm((nlocal // 2, RHS, 2 * RANK), f32),
        vm((RHS, SPAN), f32),
        vm((RANK, 6 * RANK), bf16),
        vm((RANK, 6 * RANK), bf16),
        vm((RANK, 4 * RANK), bf16),
        vm((RANK, 4 * RANK), bf16),
        vm((RANK, 4 * RANK), bf16),
        vm((RANK, 4 * RANK), bf16),
        vm((RANK, 9 * RANK), bf16),
        vm((RANK, 9 * RANK), bf16),
        vm((LEVELS, RHS, 2 * RANK), f32),
        vm((npeers, RHS, 2 * RANK), f32),
        pltpu.SemaphoreType.DMA((10,)),
        pltpu.SemaphoreType.DMA((npeers,)),
        pltpu.SemaphoreType.DMA((npeers,)),
        pltpu.SemaphoreType.DMA((2,)),
        pltpu.SemaphoreType.DMA((2,)),
    ]
    return pl.pallas_call(
        kernel,
        out_shape=jax.ShapeDtypeStruct((RHS, SPAN), f32),
        in_specs=[hbm] * 10,
        out_specs=pl.BlockSpec(memory_space=pltpu.VMEM),
        scratch_shapes=scratch,
        compiler_params=pltpu.CompilerParams(
            collective_id=0, has_side_effects=True, vmem_limit_bytes=40 * 1024 * 1024
        ),
    )(*[
        pltpu.with_memory_space_constraint(v, pltpu.HBM)
        for v in (densities, panels, areas.reshape(1, SPAN), near_offsets.T, near_count,
        leaf_basis, local_trans, local_coupling, up_trans, coupling)
    ])


def solution(mesh):
    return jax.shard_map(
        per_device,
        mesh=mesh,
        in_specs=(
            P(None, "leaf"),
            P(None, "leaf"),
            P("leaf"),
            P("leaf", None),
            P("leaf"),
            P("leaf", None, None),
            P("leaf", None, None),
            P("leaf", None, None),
            P("leaf", None, None, None),
            P("leaf", None, None, None),
        ),
        out_specs=P(None, "leaf"),
        check_vma=False,
    )
```

```python
import jax
import jax.numpy as jnp
from jax import lax
from jax.experimental import pallas as pl
from jax.experimental.pallas import tpu as pltpu
from jax.sharding import PartitionSpec as P

LEAF = 64
RANK = 64
RHS = 16
LEAVES = 32
HALO = 4
NNEAR = 6
LEVELS = 8
DEPTH = 5
NODES = 256
SPAN = LEAVES * LEAF
NOLEAF = LEAVES + 2 * HALO
softening = 0.25
MESH = pl.DeviceIdType.MESH
f32 = jnp.float32
bf16 = jnp.bfloat16

PHASES = ((0, 3), (3, 2), (5, 3))
START = [2 * LEAVES - 2 * (LEAVES >> j) for j in range(DEPTH)]
PAIR = [s // 2 for s in START]


def hops(p):
    count = 0
    for bits, size in ((p >> 1 & 3, 4), (p >> 3 & 3, 4), (p >> 5, 8)):
        count += max(min((a ^ bits) - a & size - 1, a - (a ^ bits) & size - 1) for a in range(size))
    return count


def split(x):
    high = x.astype(bf16)
    return high, (x - high.astype(f32)).astype(bf16)


def dot(a, b):
    return lax.dot_general(a, b, (((1,), (0,)), ((), ())), preferred_element_type=f32)


def dot_t(a, b):
    return lax.dot_general(a, b, (((1,), (1,)), ((), ())), preferred_element_type=f32)


def product(a, b, op):
    ah, al = a
    bh, bl = b
    rows = ah.shape[0]
    both = op(jnp.concatenate([ah, al], 0), bh)
    return both[:rows] + (both[rows:] + op(ah, bl))


def sweep(count, body, unroll):
    if count <= unroll:
        for i in range(count):
            body(i)
        return

    def step(i, carry):
        for u in range(unroll):
            body(i * unroll + u)
        return carry

    lax.fori_loop(0, count // unroll, step, 0)


def rows_at(index, count):
    if isinstance(index, int):
        return slice(index * count, (index + 1) * count)
    return pl.ds(pl.multiple_of(index * count, count), count)


def kernel(
    dens_hbm, pan_hbm, area_hbm, off_hbm, cnt_hbm, bas_hbm, ltr_hbm, lco_hbm, upt_hbm, cpl_hbm,
    out_ref,
    off_ref, cnt_ref, dens, pan, area, bas, ltr, lco, upt, cpl,
    bas_h, bas_l, ltr_h, ltr_l, gch, gcl, dt,
    coords, charge, ends, halo, column, points, qrow, gpair, hpair, acc,
    wt1h, wt1l, wt2h, wt2l, wt3h, wt3l, wk_h, wk_l,
    send, recv, load_sem, send_sem, recv_sem, halo_ssem, halo_rsem,
):
    me = lax.axis_index("leaf")
    right = lax.rem(me + 1, NODES)
    left = lax.rem(me + NODES - 1, NODES)
    loads = {}
    for at, (name, src, dst) in enumerate(
        (
            ("dens", dens_hbm, dens),
            ("bas", bas_hbm, bas),
            ("ltr", ltr_hbm, ltr),
            ("upt", upt_hbm, upt),
            ("pan", pan_hbm, pan),
            ("area", area_hbm, area),
            ("off", off_hbm, off_ref),
            ("cnt", cnt_hbm, cnt_ref),
            ("lco", lco_hbm, lco),
            ("cpl", cpl_hbm, cpl),
        )
    ):
        loads[name] = pltpu.make_async_copy(src, dst, load_sem.at[at])
        loads[name].start()

    barrier = pltpu.get_barrier_semaphore()
    peers = [p << first for first, levels in PHASES for p in range(1, 1 << levels)]
    for p in peers:
        pl.semaphore_signal(barrier, inc=1, device_id=(me ^ p,), device_id_type=MESH)
    for neighbour in (left, right):
        pl.semaphore_signal(barrier, inc=1, device_id=(neighbour,), device_id_type=MESH)

    lane = lax.broadcasted_iota(jnp.int32, (1, 2 * LEAF), 1)
    low = lane < LEAF
    half = jnp.zeros((RHS, LEAF), f32)

    loads["dens"].wait()
    loads["bas"].wait()

    def moments(p):
        x = dens[:, rows_at(p, 2 * LEAF)]
        x = jnp.concatenate([jnp.where(low, x, 0.0), jnp.where(low, 0.0, x)], 0)
        w = split(bas[rows_at(p, 2)].reshape(2 * LEAF, RANK))
        bas_h[rows_at(p, 2 * LEAF)] = w[0]
        bas_l[rows_at(p, 2 * LEAF)] = w[1]
        qrow[p] = product(split(x), w, dot)

    sweep(LEAVES // 2, moments, 16)
    loads["ltr"].wait()

    def lift(level, p):
        q = qrow[PAIR[level] + p]
        q = jnp.concatenate([q[:RHS], q[RHS:]], 1)
        at = PAIR[level] + p
        w = split(ltr[rows_at(at, 2)].reshape(2 * RANK, RANK))
        ltr_h[rows_at(at, 2 * RANK)] = w[0]
        ltr_l[rows_at(at, 2 * RANK)] = w[1]
        return product(split(q), w, dot)

    for level in range(DEPTH - 1):

        def lift_two(m, level=level):
            qrow[PAIR[level + 1] + m] = jnp.concatenate(
                [lift(level, 2 * m), lift(level, 2 * m + 1)], 0
            )

        sweep(LEAVES >> (level + 2), lift_two, 16)
    loads["upt"].wait()

    e = [split(upt[0, k]) for k in range(LEVELS - 1)]
    zero = jnp.zeros((RANK, RANK), f32)

    def chain(first, count):
        out = [upt[0, first]]
        for k in range(first + 1, first + count):
            out.append(product(split(out[-1]), e[k], dot))
        return out

    t1, t2, t3 = chain(0, 3)
    wt1h[...], wt1l[...] = split(jnp.concatenate([t3, zero, t3, t1, t3, t2], 1))
    coef = lift(DEPTH - 1, 0)

    def exchange(phase, messages):
        first, levels = PHASES[phase]
        base = sum((1 << n) - 1 for _, n in PHASES[:phase])
        slot = sum(n for _, n in PHASES[:phase])
        for k in range(levels):
            send[slot + k] = messages[k]
        copies = []
        for p in sorted(range(1, 1 << levels), key=lambda p: -hops(p << first)):
            copy = pltpu.make_async_remote_copy(
                src_ref=send.at[slot + p.bit_length() - 1],
                dst_ref=recv.at[base + p - 1],
                send_sem=send_sem.at[base + p - 1],
                recv_sem=recv_sem.at[base + p - 1],
                device_id=(me ^ (p << first),),
                device_id_type=MESH,
            )
            copy.start()
            copies.append(copy)

        def receive():
            for copy in copies:
                copy.wait()
            sums = []
            for k in range(levels):
                parts = [recv[base + p - 1] for p in range(1 << k, 2 << k)]
                while len(parts) > 1:
                    parts = [a + b for a, b in zip(parts[::2], parts[1::2])]
                sums.append(parts[0])
            return sums

        return receive

    own = product(split(coef), (wt1h[...], wt1l[...]), dot)
    own = [own[:, 2 * RANK * k : 2 * RANK * (k + 1)] for k in range(3)]
    own[0] = own[0] + jnp.concatenate([half, coef], 1)
    pl.semaphore_wait(barrier, len(peers) + 2)
    receive = exchange(0, own)

    loads["pan"].wait()
    loads["area"].wait()
    halo_rows = jnp.zeros((5, 2 * LEAF), f32)

    def place(tile, slot):
        coords[slot] = tile[RHS:]
        coords[slot + 1] = pltpu.roll(tile[RHS:], LEAF, 1)
        high, rest = split(tile[:RHS].T)
        charge[pl.ds(slot, 2)] = jnp.concatenate([high, rest], 1).reshape(2, LEAF, 2 * RHS)

    def pack(p):
        at = rows_at(p, 2 * LEAF)
        where = jnp.concatenate([pan[:, at], halo_rows], 0)
        tile = jnp.concatenate([dens[:, at] * area[:, at], where], 0)
        if p in (0, 1, 14, 15):
            ends[p if p < 2 else p - 12] = tile
        place(tile, HALO + 2 * p)
        points[at, :] = where.T

    for p in (0, 1, 14, 15):
        pack(p)
    halos = []
    for at, (source, target, device) in enumerate(((2, 0, right), (0, 2, left))):
        copy = pltpu.make_async_remote_copy(
            src_ref=ends.at[pl.ds(source, 2)],
            dst_ref=halo.at[pl.ds(target, 2)],
            send_sem=halo_ssem.at[at],
            recv_sem=halo_rsem.at[at],
            device_id=(device,),
            device_id_type=MESH,
        )
        copy.start()
        halos.append(copy)
    for p in range(2, 14):
        pack(p)
    coords[NOLEAF] = jnp.zeros((8, 2 * LEAF), f32)
    coords[NOLEAF + 1] = jnp.zeros((8, 2 * LEAF), f32)
    charge[NOLEAF] = jnp.zeros((LEAF, 2 * RHS), bf16)

    u4, u5 = chain(3, 2)
    wt2h[...], wt2l[...] = split(jnp.concatenate([u5, zero, u5, u4], 1))
    v6, v7 = chain(5, 2)
    wt3h[...], wt3l[...] = split(jnp.concatenate([zero, v6, v7, zero], 1))
    loads["cpl"].wait()
    t4 = product(split(t3), e[3], dot)
    t5 = product(split(t3), split(u5), dot)
    t6 = product(split(t5), e[5], dot)
    t7 = product(split(t5), split(v7), dot)
    blank = jnp.zeros((2 * RANK, RANK), bf16)
    wk_h[:, rows_at(LEVELS, RANK)] = blank
    wk_l[:, rows_at(LEVELS, RANK)] = blank
    for k, t in enumerate((None, t1, t2, t3, t4, t5, t6, t7)):
        w = cpl[0, k] if t is None else product(split(t), split(cpl[0, k]), dot)
        wk_h[:, rows_at(k, RANK)], wk_l[:, rows_at(k, RANK)] = split(jnp.concatenate([w, w], 0))

    loads["lco"].wait()

    def couple(p):
        q = qrow[p]
        q = jnp.concatenate([q[RHS:], q[:RHS]], 0)
        w = split(lco[rows_at(p, 2)].reshape(2 * RANK, RANK))
        g = product(split(q), w, dot_t)
        gpair[p] = jnp.where(low, g[:RHS], g[RHS:])

    sweep(28, couple, 14)
    for p in range(28, 31):
        couple(p)

    sums = receive()
    tot = own[0] + (sums[0] + (sums[1] + sums[2]))
    coef = tot[:, :RANK]
    early = [s[:, RANK:] for s in sums]
    own = product(split(coef), (wt2h[...], wt2l[...]), dot)
    own = [own[:, 2 * RANK * k : 2 * RANK * (k + 1)] for k in range(2)]
    own[0] = own[0] + jnp.concatenate([half, coef], 1)
    receive = exchange(1, own)

    hpair[PAIR[4]] = gpair[PAIR[4]]

    for level in range(DEPTH - 2, -1, -1):

        def lower_two(m, level=level):
            parent = hpair[PAIR[level + 1] + m]
            for c in range(2):
                at = PAIR[level] + 2 * m + c
                w = (ltr_h[rows_at(at, 2 * RANK)], ltr_l[rows_at(at, 2 * RANK)])
                h = split(parent[:, RANK * c : RANK * (c + 1)])
                hpair[at] = gpair[at] + product(h, w, dot_t)

        sweep(LEAVES >> (level + 2), lower_two, 16)

    def far_leaf(p):
        h = hpair[p]
        h = jnp.concatenate([h[:, :RANK], h[:, RANK:]], 0)
        w = (bas_h[rows_at(p, 2 * LEAF)], bas_l[rows_at(p, 2 * LEAF)])
        far = product(split(h), w, dot_t)
        acc[:, rows_at(p, 2 * LEAF)] = jnp.where(low, far[:RHS], far[RHS:])

    sweep(LEAVES // 2, far_leaf, 16)

    loads["off"].wait()
    loads["cnt"].wait()
    for copy in halos:
        copy.wait()
    for end, slot, edge in ((0, 0, 0), (2, HALO + LEAVES, NODES - 1)):
        keep = jnp.where(me == edge, 0.0, 1.0)
        for t in range(2):
            place(halo[end + t] * keep, slot + 2 * t)

    def near_leaf(i):
        at = rows_at(i, LEAF)
        tx, ty, tz = (jnp.broadcast_to(points[at, c : c + 1], (LEAF, 2 * LEAF)) for c in range(3))
        count = cnt_ref[i]
        kernels, charges = [], []
        for t in range(NNEAR // 2):
            j = [
                jnp.where(s < count, off_ref[s, i] + (i + HALO), NOLEAF)
                for s in (2 * t, 2 * t + 1)
            ]
            charges += [charge[j[0]], charge[j[1]]]
            c = jnp.where(low, coords[j[0]], coords[j[1] ^ 1])
            dx = tx - c[0:1]
            dy = ty - c[1:2]
            dz = tz - c[2:3]
            kernels.append(lax.rsqrt(dx * dx + dy * dy + (dz * dz + softening)))
        high, rest = split(jnp.concatenate(kernels, 1))
        both = dot(jnp.concatenate([high, rest], 0), jnp.concatenate(charges, 0))
        column[at, :] = both[:LEAF] + both[LEAF:]

    def near(p):
        near_leaf(2 * p)
        near_leaf(2 * p + 1)

    def near_fold(p):
        at = rows_at(p, 2 * LEAF)
        tile = column[at, :].T
        acc[:, at] = acc[:, at] + (tile[:RHS] + tile[RHS:])

    def near_some(first, last):
        sweep(last - first, lambda p: near(p + first), 4)

    near_some(0, 8)

    sums = receive()
    tot = own[0] + (sums[0] + sums[1])
    coef = tot[:, :RANK]
    early += [s[:, RANK:] for s in sums]
    own = product(split(coef), (wt3h[...], wt3l[...]), dot)
    own = [jnp.concatenate([coef, half], 1), own[:, : 2 * RANK], own[:, 2 * RANK :]]
    receive = exchange(2, own)

    local = jnp.zeros((RHS, 2 * RANK), f32)
    for k in range(5):
        w = (wk_h[:, rows_at(k, RANK)], wk_l[:, rows_at(k, RANK)])
        local = local + product(split(early[k]), w, dot_t)

    top = rows_at(PAIR[4], 2 * RANK)
    gch[top] = ltr_h[top]
    gcl[top] = ltr_l[top]
    for level in range(DEPTH - 2, -1, -1):

        def compose(m, level=level):
            at = rows_at(PAIR[level] + m, 2 * RANK)
            up = rows_at(START[level + 1] + m, RANK)
            gch[at], gcl[at] = split(
                product((ltr_h[at], ltr_l[at]), (gch[up], gcl[up]), dot)
            )

        sweep(LEAVES >> (level + 1), compose, 16)

    def compose_leaf(p):
        pair = []
        for i in (2 * p, 2 * p + 1):
            at = rows_at(i, LEAF)
            pair.append(product((bas_h[at], bas_l[at]), (gch[at], gcl[at]), dot))
        high, rest = split(jnp.concatenate(pair, 0).T)
        dt[:, rows_at(p, 2 * LEAF)] = jnp.concatenate([high, rest], 0)

    sweep(LEAVES // 2, compose_leaf, 8)
    near_some(8, 16)
    for p in range(LEAVES // 2):
        near_fold(p)

    s5, s6, s7 = receive()
    tail = split(jnp.concatenate([s5 + s6, s7], 1))
    w = (wk_h[:, 5 * RANK :], wk_l[:, 5 * RANK :])
    high, rest = split(local + product(tail, w, dot_t))
    rest = jnp.where(low, rest.astype(f32), 0.0).astype(bf16)
    local = jnp.concatenate([high, rest], 0)
    for b in range(4):
        at = rows_at(b, 512)
        far = dot(local, dt[:, at])
        out_ref[:, at] = acc[:, at] + (far[:RHS] + far[RHS:])


def per_device(
    densities, panels, areas, near_offsets, near_count,
    leaf_basis, local_trans, local_coupling, up_trans, coupling,
):
    hbm = pl.BlockSpec(memory_space=pltpu.HBM)
    nlocal = 2 * LEAVES - 2
    npeers = sum((1 << n) - 1 for _, n in PHASES)
    vm = pltpu.VMEM
    scratch = [
        pltpu.SMEM((NNEAR, LEAVES), jnp.int32),
        pltpu.SMEM((LEAVES,), jnp.int32),
        vm((RHS, SPAN), f32),
        vm((3, SPAN), f32),
        vm((1, SPAN), f32),
        vm((LEAVES, LEAF, RANK), f32),
        vm((nlocal, RANK, RANK), f32),
        vm((nlocal, RANK, RANK), f32),
        vm((1, LEVELS, RANK, RANK), f32),
        vm((1, LEVELS, RANK, RANK), f32),
        vm((SPAN, RANK), bf16),
        vm((SPAN, RANK), bf16),
        vm((nlocal * RANK, RANK), bf16),
        vm((nlocal * RANK, RANK), bf16),
        vm((nlocal * RANK, RANK), bf16),
        vm((nlocal * RANK, RANK), bf16),
        vm((2 * RANK, SPAN), bf16),
        vm((NOLEAF + 2, 8, 2 * LEAF), f32),
        vm((NOLEAF + 1, LEAF, 2 * RHS), bf16),
        vm((4, RHS + 8, 2 * LEAF), f32),
        vm((4, RHS + 8, 2 * LEAF), f32),
        vm((SPAN, 2 * RHS), f32),
        vm((SPAN, 8), f32),
        vm((nlocal // 2, 2 * RHS, RANK), f32),
        vm((nlocal // 2, RHS, 2 * RANK), f32),
        vm((nlocal // 2, RHS, 2 * RANK), f32),
        vm((RHS, SPAN), f32),
        vm((RANK, 6 * RANK), bf16),
        vm((RANK, 6 * RANK), bf16),
        vm((RANK, 4 * RANK), bf16),
        vm((RANK, 4 * RANK), bf16),
        vm((RANK, 4 * RANK), bf16),
        vm((RANK, 4 * RANK), bf16),
        vm((2 * RANK, 9 * RANK), bf16),
        vm((2 * RANK, 9 * RANK), bf16),
        vm((LEVELS, RHS, 2 * RANK), f32),
        vm((npeers, RHS, 2 * RANK), f32),
        pltpu.SemaphoreType.DMA((10,)),
        pltpu.SemaphoreType.DMA((npeers,)),
        pltpu.SemaphoreType.DMA((npeers,)),
        pltpu.SemaphoreType.DMA((2,)),
        pltpu.SemaphoreType.DMA((2,)),
    ]
    return pl.pallas_call(
        kernel,
        out_shape=jax.ShapeDtypeStruct((RHS, SPAN), f32),
        in_specs=[hbm] * 10,
        out_specs=pl.BlockSpec(memory_space=pltpu.VMEM),
        scratch_shapes=scratch,
        compiler_params=pltpu.CompilerParams(
            collective_id=0, has_side_effects=True, vmem_limit_bytes=40 * 1024 * 1024
        ),
    )(*[
        pltpu.with_memory_space_constraint(v, pltpu.HBM)
        for v in (densities, panels, areas.reshape(1, SPAN), near_offsets.T, near_count,
        leaf_basis, local_trans, local_coupling, up_trans, coupling)
    ])


def solution(mesh):
    return jax.shard_map(
        per_device,
        mesh=mesh,
        in_specs=(
            P(None, "leaf"),
            P(None, "leaf"),
            P("leaf"),
            P("leaf", None),
            P("leaf"),
            P("leaf", None, None),
            P("leaf", None, None),
            P("leaf", None, None),
            P("leaf", None, None, None),
            P("leaf", None, None, None),
        ),
        out_specs=P(None, "leaf"),
        check_vma=False,
    )
```

```python
import jax
import jax.numpy as jnp
from jax import lax
from jax.experimental import pallas as pl
from jax.experimental.pallas import tpu as pltpu
from jax.sharding import PartitionSpec as P

LEAF = 64
RANK = 64
RHS = 16
LEAVES = 32
HALO = 4
NNEAR = 6
LEVELS = 8
DEPTH = 5
NODES = 256
SPAN = LEAVES * LEAF
NOLEAF = LEAVES + 2 * HALO
softening = 0.25
MESH = pl.DeviceIdType.MESH
f32 = jnp.float32
bf16 = jnp.bfloat16

PHASES = ((0, 3), (3, 2), (5, 3))
START = [2 * LEAVES - 2 * (LEAVES >> j) for j in range(DEPTH)]
PAIR = [s // 2 for s in START]


def hops(p):
    count = 0
    for bits, size in ((p >> 1 & 3, 4), (p >> 3 & 3, 4), (p >> 5, 8)):
        count += max(min((a ^ bits) - a & size - 1, a - (a ^ bits) & size - 1) for a in range(size))
    return count


def split(x):
    high = x.astype(bf16)
    return high, (x - high.astype(f32)).astype(bf16)


def dot(a, b):
    return lax.dot_general(a, b, (((1,), (0,)), ((), ())), preferred_element_type=f32)


def dot_t(a, b):
    return lax.dot_general(a, b, (((1,), (1,)), ((), ())), preferred_element_type=f32)


def product(a, b, op):
    ah, al = a
    bh, bl = b
    rows = ah.shape[0]
    both = op(jnp.concatenate([ah, al], 0), bh)
    return both[:rows] + (both[rows:] + op(ah, bl))


def sweep(count, body, unroll):
    if count <= unroll:
        for i in range(count):
            body(i)
        return

    def step(i, carry):
        for u in range(unroll):
            body(i * unroll + u)
        return carry

    lax.fori_loop(0, count // unroll, step, 0)


def rows_at(index, count):
    if isinstance(index, int):
        return slice(index * count, (index + 1) * count)
    return pl.ds(pl.multiple_of(index * count, count), count)


def kernel(
    dens_hbm, pan_hbm, area_hbm, off_hbm, cnt_hbm, bas_hbm, ltr_hbm, lco_hbm, upt_hbm, cpl_hbm,
    out_ref,
    off_ref, cnt_ref, dens, pan, area, bas, ltr, lco, upt, cpl,
    bas_h, bas_l, ltr_h, ltr_l, gch, gcl, dt,
    coords, charge, ends, halo, column, points, qrow, gpair, hpair, acc,
    wt1h, wt1l, wt2h, wt2l, wt3h, wt3l, wk_h, wk_l,
    send, recv, load_sem, send_sem, recv_sem, halo_ssem, halo_rsem,
):
    me = lax.axis_index("leaf")
    right = lax.rem(me + 1, NODES)
    left = lax.rem(me + NODES - 1, NODES)
    loads = {}
    for at, (name, src, dst) in enumerate(
        (
            ("dens", dens_hbm, dens),
            ("bas", bas_hbm, bas),
            ("ltr", ltr_hbm.at[pl.ds(0, 32)], ltr.at[pl.ds(0, 32)]),
            ("ltu", ltr_hbm.at[pl.ds(32, 30)], ltr.at[pl.ds(32, 30)]),
            ("upt", upt_hbm, upt),
            ("pan", pan_hbm, pan),
            ("area", area_hbm, area),
            ("off", off_hbm, off_ref),
            ("cnt", cnt_hbm, cnt_ref),
            ("lco", lco_hbm, lco),
            ("cpl", cpl_hbm, cpl),
        )
    ):
        loads[name] = pltpu.make_async_copy(src, dst, load_sem.at[at])
        loads[name].start()

    barrier = pltpu.get_barrier_semaphore()
    peers = [p << first for first, levels in PHASES for p in range(1, 1 << levels)]
    for p in peers:
        pl.semaphore_signal(barrier, inc=1, device_id=(me ^ p,), device_id_type=MESH)
    for neighbour in (left, right):
        pl.semaphore_signal(barrier, inc=1, device_id=(neighbour,), device_id_type=MESH)

    lane = lax.broadcasted_iota(jnp.int32, (1, 2 * LEAF), 1)
    low = lane < LEAF
    half = jnp.zeros((RHS, LEAF), f32)

    loads["dens"].wait()
    loads["bas"].wait()

    def moments(p):
        x = dens[:, rows_at(p, 2 * LEAF)]
        x = jnp.concatenate([jnp.where(low, x, 0.0), jnp.where(low, 0.0, x)], 0)
        w = split(bas[rows_at(p, 2)].reshape(2 * LEAF, RANK))
        bas_h[rows_at(p, 2 * LEAF)] = w[0]
        bas_l[rows_at(p, 2 * LEAF)] = w[1]
        qrow[p] = product(split(x), w, dot)

    sweep(LEAVES // 2, moments, 16)
    loads["ltr"].wait()

    def lift(level, p):
        q = qrow[PAIR[level] + p]
        q = jnp.concatenate([q[:RHS], q[RHS:]], 1)
        at = PAIR[level] + p
        w = split(ltr[rows_at(at, 2)].reshape(2 * RANK, RANK))
        ltr_h[rows_at(at, 2 * RANK)] = w[0]
        ltr_l[rows_at(at, 2 * RANK)] = w[1]
        return product(split(q), w, dot)

    for level in range(DEPTH - 1):
        if level == 1:
            loads["ltu"].wait()

        def lift_two(m, level=level):
            qrow[PAIR[level + 1] + m] = jnp.concatenate(
                [lift(level, 2 * m), lift(level, 2 * m + 1)], 0
            )

        sweep(LEAVES >> (level + 2), lift_two, 16)
    loads["upt"].wait()

    e = [split(upt[0, k]) for k in range(LEVELS - 1)]
    zero = jnp.zeros((RANK, RANK), f32)

    def chain(first, count):
        out = [upt[0, first]]
        for k in range(first + 1, first + count):
            out.append(product(split(out[-1]), e[k], dot))
        return out

    t1, t2, t3 = chain(0, 3)
    wt1h[...], wt1l[...] = split(jnp.concatenate([t3, zero, t3, t1, t3, t2], 1))
    coef = lift(DEPTH - 1, 0)

    pending = []

    def exchange(phase, messages):
        first, levels = PHASES[phase]
        base = sum((1 << n) - 1 for _, n in PHASES[:phase])
        slot = sum(n for _, n in PHASES[:phase])
        for k in range(levels):
            send[slot + k] = messages[k]
        copies = []
        for p in sorted(range(1, 1 << levels), key=lambda p: -hops(p << first)):
            copy = pltpu.make_async_remote_copy(
                src_ref=send.at[slot + p.bit_length() - 1],
                dst_ref=recv.at[base + p - 1],
                send_sem=send_sem.at[base + p - 1],
                recv_sem=recv_sem.at[base + p - 1],
                device_id=(me ^ (p << first),),
                device_id_type=MESH,
            )
            copy.start()
            copies.append(copy)

        def receive():
            for copy in copies:
                copy.wait_recv()
            pending.extend(copies)
            sums = []
            for k in range(levels):
                parts = [recv[base + p - 1] for p in range(1 << k, 2 << k)]
                while len(parts) > 1:
                    parts = [a + b for a, b in zip(parts[::2], parts[1::2])]
                sums.append(parts[0])
            return sums

        return receive

    own = product(split(coef), (wt1h[...], wt1l[...]), dot)
    own = [own[:, 2 * RANK * k : 2 * RANK * (k + 1)] for k in range(3)]
    own[0] = own[0] + jnp.concatenate([half, coef], 1)
    pl.semaphore_wait(barrier, len(peers) + 2)
    receive = exchange(0, own)

    loads["pan"].wait()
    loads["area"].wait()
    halo_rows = jnp.zeros((5, 2 * LEAF), f32)

    def place(tile, slot):
        coords[slot] = tile[RHS:]
        coords[slot + 1] = pltpu.roll(tile[RHS:], LEAF, 1)
        high, rest = split(tile[:RHS].T)
        charge[pl.ds(slot, 2)] = jnp.concatenate([high, rest], 1).reshape(2, LEAF, 2 * RHS)

    def pack(p):
        at = rows_at(p, 2 * LEAF)
        where = jnp.concatenate([pan[:, at], halo_rows], 0)
        tile = jnp.concatenate([dens[:, at] * area[:, at], where], 0)
        if p in (0, 1, 14, 15):
            ends[p if p < 2 else p - 12] = tile
        place(tile, HALO + 2 * p)
        points[at, :] = where.T

    for p in (0, 1, 14, 15):
        pack(p)
    halos = []
    for at, (source, target, device) in enumerate(((2, 0, right), (0, 2, left))):
        copy = pltpu.make_async_remote_copy(
            src_ref=ends.at[pl.ds(source, 2)],
            dst_ref=halo.at[pl.ds(target, 2)],
            send_sem=halo_ssem.at[at],
            recv_sem=halo_rsem.at[at],
            device_id=(device,),
            device_id_type=MESH,
        )
        copy.start()
        halos.append(copy)
    for p in range(2, 14):
        pack(p)
    coords[NOLEAF] = jnp.zeros((8, 2 * LEAF), f32)
    coords[NOLEAF + 1] = jnp.zeros((8, 2 * LEAF), f32)
    charge[NOLEAF] = jnp.zeros((LEAF, 2 * RHS), bf16)

    u4, u5 = chain(3, 2)
    wt2h[...], wt2l[...] = split(jnp.concatenate([u5, zero, u5, u4], 1))
    v6, v7 = chain(5, 2)
    wt3h[...], wt3l[...] = split(jnp.concatenate([zero, v6, v7, zero], 1))
    loads["cpl"].wait()
    t4 = product(split(t3), e[3], dot)
    t5 = product(split(t3), split(u5), dot)
    t6 = product(split(t5), e[5], dot)
    t7 = product(split(t5), split(v7), dot)
    blank = jnp.zeros((2 * RANK, RANK), bf16)
    wk_h[:, rows_at(LEVELS, RANK)] = blank
    wk_l[:, rows_at(LEVELS, RANK)] = blank
    for k, t in enumerate((None, t1, t2, t3, t4, t5, t6, t7)):
        w = cpl[0, k] if t is None else product(split(t), split(cpl[0, k]), dot)
        wk_h[:, rows_at(k, RANK)], wk_l[:, rows_at(k, RANK)] = split(jnp.concatenate([w, w], 0))

    loads["lco"].wait()

    def couple(p):
        q = qrow[p]
        q = jnp.concatenate([q[RHS:], q[:RHS]], 0)
        w = split(lco[rows_at(p, 2)].reshape(2 * RANK, RANK))
        g = product(split(q), w, dot_t)
        gpair[p] = jnp.where(low, g[:RHS], g[RHS:])

    sweep(28, couple, 14)
    for p in range(28, 31):
        couple(p)

    sums = receive()
    tot = own[0] + (sums[0] + (sums[1] + sums[2]))
    coef = tot[:, :RANK]
    early = [s[:, RANK:] for s in sums]
    own = product(split(coef), (wt2h[...], wt2l[...]), dot)
    own = [own[:, 2 * RANK * k : 2 * RANK * (k + 1)] for k in range(2)]
    own[0] = own[0] + jnp.concatenate([half, coef], 1)
    receive = exchange(1, own)

    hpair[PAIR[4]] = gpair[PAIR[4]]

    for level in range(DEPTH - 2, -1, -1):

        def lower_two(m, level=level):
            parent = hpair[PAIR[level + 1] + m]
            for c in range(2):
                at = PAIR[level] + 2 * m + c
                w = (ltr_h[rows_at(at, 2 * RANK)], ltr_l[rows_at(at, 2 * RANK)])
                h = split(parent[:, RANK * c : RANK * (c + 1)])
                hpair[at] = gpair[at] + product(h, w, dot_t)

        sweep(LEAVES >> (level + 2), lower_two, 16)

    def far_leaf(p):
        h = hpair[p]
        h = jnp.concatenate([h[:, :RANK], h[:, RANK:]], 0)
        w = (bas_h[rows_at(p, 2 * LEAF)], bas_l[rows_at(p, 2 * LEAF)])
        far = product(split(h), w, dot_t)
        acc[:, rows_at(p, 2 * LEAF)] = jnp.where(low, far[:RHS], far[RHS:])

    sweep(LEAVES // 2, far_leaf, 16)

    loads["off"].wait()
    loads["cnt"].wait()
    for copy in halos:
        copy.wait()
    for end, slot, edge in ((0, 0, 0), (2, HALO + LEAVES, NODES - 1)):
        keep = jnp.where(me == edge, 0.0, 1.0)
        for t in range(2):
            place(halo[end + t] * keep, slot + 2 * t)

    def near_leaf(i):
        at = rows_at(i, LEAF)
        tx, ty, tz = (jnp.broadcast_to(points[at, c : c + 1], (LEAF, 2 * LEAF)) for c in range(3))
        count = cnt_ref[i]
        kernels, charges = [], []
        for t in range(NNEAR // 2):
            j = [
                jnp.where(s < count, off_ref[s, i] + (i + HALO), NOLEAF)
                for s in (2 * t, 2 * t + 1)
            ]
            charges += [charge[j[0]], charge[j[1]]]
            c = jnp.where(low, coords[j[0]], coords[j[1] ^ 1])
            dx = tx - c[0:1]
            dy = ty - c[1:2]
            dz = tz - c[2:3]
            kernels.append(lax.rsqrt(dx * dx + dy * dy + (dz * dz + softening)))
        high, rest = split(jnp.concatenate(kernels, 1))
        both = dot(jnp.concatenate([high, rest], 0), jnp.concatenate(charges, 0))
        column[at, :] = both[:LEAF] + both[LEAF:]

    def near(p):
        near_leaf(2 * p)
        near_leaf(2 * p + 1)

    def near_fold(p):
        at = rows_at(p, 2 * LEAF)
        tile = column[at, :].T
        acc[:, at] = acc[:, at] + (tile[:RHS] + tile[RHS:])

    def near_some(first, last):
        sweep(last - first, lambda p: near(p + first), 4)

    near_some(0, 8)

    sums = receive()
    tot = own[0] + (sums[0] + sums[1])
    coef = tot[:, :RANK]
    early += [s[:, RANK:] for s in sums]
    own = product(split(coef), (wt3h[...], wt3l[...]), dot)
    own = [jnp.concatenate([coef, half], 1), own[:, : 2 * RANK], own[:, 2 * RANK :]]
    receive = exchange(2, own)

    local = jnp.zeros((RHS, 2 * RANK), f32)
    for k in range(5):
        w = (wk_h[:, rows_at(k, RANK)], wk_l[:, rows_at(k, RANK)])
        local = local + product(split(early[k]), w, dot_t)

    top = rows_at(PAIR[4], 2 * RANK)
    gch[top] = ltr_h[top]
    gcl[top] = ltr_l[top]
    for level in range(DEPTH - 2, -1, -1):

        def compose(m, level=level):
            at = rows_at(PAIR[level] + m, 2 * RANK)
            up = rows_at(START[level + 1] + m, RANK)
            gch[at], gcl[at] = split(
                product((ltr_h[at], ltr_l[at]), (gch[up], gcl[up]), dot)
            )

        sweep(LEAVES >> (level + 1), compose, 16)

    def compose_leaf(p):
        pair = []
        for i in (2 * p, 2 * p + 1):
            at = rows_at(i, LEAF)
            pair.append(product((bas_h[at], bas_l[at]), (gch[at], gcl[at]), dot))
        high, rest = split(jnp.concatenate(pair, 0).T)
        dt[:, rows_at(p, 2 * LEAF)] = jnp.concatenate([high, rest], 0)

    sweep(LEAVES // 2, compose_leaf, 8)
    near_some(8, 16)
    for p in range(LEAVES // 2):
        near_fold(p)

    s5, s6, s7 = receive()
    tail = split(jnp.concatenate([s5 + s6, s7], 1))
    w = (wk_h[:, 5 * RANK :], wk_l[:, 5 * RANK :])
    for copy in pending:
        copy.wait_send()
    high, rest = split(local + product(tail, w, dot_t))
    rest = jnp.where(low, rest.astype(f32), 0.0).astype(bf16)
    local = jnp.concatenate([high, rest], 0)
    for b in range(4):
        at = rows_at(b, 512)
        far = dot(local, dt[:, at])
        out_ref[:, at] = acc[:, at] + (far[:RHS] + far[RHS:])


def per_device(
    densities, panels, areas, near_offsets, near_count,
    leaf_basis, local_trans, local_coupling, up_trans, coupling,
):
    hbm = pl.BlockSpec(memory_space=pltpu.HBM)
    nlocal = 2 * LEAVES - 2
    npeers = sum((1 << n) - 1 for _, n in PHASES)
    vm = pltpu.VMEM
    scratch = [
        pltpu.SMEM((NNEAR, LEAVES), jnp.int32),
        pltpu.SMEM((LEAVES,), jnp.int32),
        vm((RHS, SPAN), f32),
        vm((3, SPAN), f32),
        vm((1, SPAN), f32),
        vm((LEAVES, LEAF, RANK), f32),
        vm((nlocal, RANK, RANK), f32),
        vm((nlocal, RANK, RANK), f32),
        vm((1, LEVELS, RANK, RANK), f32),
        vm((1, LEVELS, RANK, RANK), f32),
        vm((SPAN, RANK), bf16),
        vm((SPAN, RANK), bf16),
        vm((nlocal * RANK, RANK), bf16),
        vm((nlocal * RANK, RANK), bf16),
        vm((nlocal * RANK, RANK), bf16),
        vm((nlocal * RANK, RANK), bf16),
        vm((2 * RANK, SPAN), bf16),
        vm((NOLEAF + 2, 8, 2 * LEAF), f32),
        vm((NOLEAF + 1, LEAF, 2 * RHS), bf16),
        vm((4, RHS + 8, 2 * LEAF), f32),
        vm((4, RHS + 8, 2 * LEAF), f32),
        vm((SPAN, 2 * RHS), f32),
        vm((SPAN, 8), f32),
        vm((nlocal // 2, 2 * RHS, RANK), f32),
        vm((nlocal // 2, RHS, 2 * RANK), f32),
        vm((nlocal // 2, RHS, 2 * RANK), f32),
        vm((RHS, SPAN), f32),
        vm((RANK, 6 * RANK), bf16),
        vm((RANK, 6 * RANK), bf16),
        vm((RANK, 4 * RANK), bf16),
        vm((RANK, 4 * RANK), bf16),
        vm((RANK, 4 * RANK), bf16),
        vm((RANK, 4 * RANK), bf16),
        vm((2 * RANK, 9 * RANK), bf16),
        vm((2 * RANK, 9 * RANK), bf16),
        vm((LEVELS, RHS, 2 * RANK), f32),
        vm((npeers, RHS, 2 * RANK), f32),
        pltpu.SemaphoreType.DMA((11,)),
        pltpu.SemaphoreType.DMA((npeers,)),
        pltpu.SemaphoreType.DMA((npeers,)),
        pltpu.SemaphoreType.DMA((2,)),
        pltpu.SemaphoreType.DMA((2,)),
    ]
    return pl.pallas_call(
        kernel,
        out_shape=jax.ShapeDtypeStruct((RHS, SPAN), f32),
        in_specs=[hbm] * 10,
        out_specs=pl.BlockSpec(memory_space=pltpu.VMEM),
        scratch_shapes=scratch,
        compiler_params=pltpu.CompilerParams(
            collective_id=0, has_side_effects=True, vmem_limit_bytes=40 * 1024 * 1024
        ),
    )(*[
        pltpu.with_memory_space_constraint(v, pltpu.HBM)
        for v in (densities, panels, areas.reshape(1, SPAN), near_offsets.T, near_count,
        leaf_basis, local_trans, local_coupling, up_trans, coupling)
    ])


def solution(mesh):
    return jax.shard_map(
        per_device,
        mesh=mesh,
        in_specs=(
            P(None, "leaf"),
            P(None, "leaf"),
            P("leaf"),
            P("leaf", None),
            P("leaf"),
            P("leaf", None, None),
            P("leaf", None, None),
            P("leaf", None, None),
            P("leaf", None, None, None),
            P("leaf", None, None, None),
        ),
        out_specs=P(None, "leaf"),
        check_vma=False,
    )
```

```python
import jax
import jax.numpy as jnp
from jax import lax
from jax.experimental import pallas as pl
from jax.experimental.pallas import tpu as pltpu
from jax.sharding import PartitionSpec as P

LEAF = 64
RANK = 64
RHS = 16
LEAVES = 32
HALO = 4
NNEAR = 6
LEVELS = 8
DEPTH = 5
NODES = 256
SPAN = LEAVES * LEAF
NOLEAF = LEAVES + 2 * HALO
softening = 0.25
MESH = pl.DeviceIdType.MESH
f32 = jnp.float32
bf16 = jnp.bfloat16

PHASES = ((0, 3), (3, 2), (5, 3))
START = [2 * LEAVES - 2 * (LEAVES >> j) for j in range(DEPTH)]
PAIR = [s // 2 for s in START]


def hops(p):
    count = 0
    for bits, size in ((p >> 1 & 3, 4), (p >> 3 & 3, 4), (p >> 5, 8)):
        count += max(min((a ^ bits) - a & size - 1, a - (a ^ bits) & size - 1) for a in range(size))
    return count


def split(x):
    high = x.astype(bf16)
    return high, (x - high.astype(f32)).astype(bf16)


def dot(a, b):
    return lax.dot_general(a, b, (((1,), (0,)), ((), ())), preferred_element_type=f32)


def dot_t(a, b):
    return lax.dot_general(a, b, (((1,), (1,)), ((), ())), preferred_element_type=f32)


def product(a, b, op):
    ah, al = a
    bh, bl = b
    rows = ah.shape[0]
    both = op(jnp.concatenate([ah, al], 0), bh)
    return both[:rows] + (both[rows:] + op(ah, bl))


def sweep(count, body, unroll):
    if count <= unroll:
        for i in range(count):
            body(i)
        return

    def step(i, carry):
        for u in range(unroll):
            body(i * unroll + u)
        return carry

    lax.fori_loop(0, count // unroll, step, 0)


def rows_at(index, count):
    if isinstance(index, int):
        return slice(index * count, (index + 1) * count)
    return pl.ds(pl.multiple_of(index * count, count), count)


def kernel(
    dens_hbm, pan_hbm, area_hbm, off_hbm, cnt_hbm, bas_hbm, ltr_hbm, lco_hbm, upt_hbm, cpl_hbm,
    out_ref,
    off_ref, cnt_ref, dens, pan, area, bas, ltr, lco, upt, cpl,
    bas_h, bas_l, ltr_h, ltr_l, gch, gcl, dt,
    coords, charge, ends, halo, column, points, qrow, gpair, hpair, acc,
    wt1h, wt1l, wt2h, wt2l, wt3h, wt3l, wk_h, wk_l,
    send, recv, load_sem, send_sem, recv_sem, halo_ssem, halo_rsem,
):
    me = lax.axis_index("leaf")
    right = lax.rem(me + 1, NODES)
    left = lax.rem(me + NODES - 1, NODES)
    loads = {}
    for at, (name, src, dst) in enumerate(
        (
            ("dens", dens_hbm, dens),
            ("bas", bas_hbm, bas),
            ("ltr", ltr_hbm.at[pl.ds(0, 32)], ltr.at[pl.ds(0, 32)]),
            ("ltu", ltr_hbm.at[pl.ds(32, 30)], ltr.at[pl.ds(32, 30)]),
            ("upt", upt_hbm, upt),
            ("pan", pan_hbm, pan),
            ("area", area_hbm, area),
            ("off", off_hbm, off_ref),
            ("cnt", cnt_hbm, cnt_ref),
            ("lco", lco_hbm, lco),
            ("cpl", cpl_hbm, cpl),
        )
    ):
        loads[name] = pltpu.make_async_copy(src, dst, load_sem.at[at])
        loads[name].start()

    barrier = pltpu.get_barrier_semaphore()
    peers = [p << first for first, levels in PHASES for p in range(1, 1 << levels)]
    for p in peers:
        pl.semaphore_signal(barrier, inc=1, device_id=(me ^ p,), device_id_type=MESH)
    for neighbour in (left, right):
        pl.semaphore_signal(barrier, inc=1, device_id=(neighbour,), device_id_type=MESH)

    lane = lax.broadcasted_iota(jnp.int32, (1, 2 * LEAF), 1)
    low = lane < LEAF
    half = jnp.zeros((RHS, LEAF), f32)

    loads["dens"].wait()
    loads["bas"].wait()

    def moments(p):
        x = dens[:, rows_at(p, 2 * LEAF)]
        x = jnp.concatenate([jnp.where(low, x, 0.0), jnp.where(low, 0.0, x)], 0)
        w = split(bas[rows_at(p, 2)].reshape(2 * LEAF, RANK))
        bas_h[rows_at(p, 2 * LEAF)] = w[0]
        bas_l[rows_at(p, 2 * LEAF)] = w[1]
        qrow[p] = product(split(x), w, dot)

    sweep(LEAVES // 2, moments, 16)
    loads["ltr"].wait()

    def lift(level, p):
        q = qrow[PAIR[level] + p]
        q = jnp.concatenate([q[:RHS], q[RHS:]], 1)
        at = PAIR[level] + p
        w = split(ltr[rows_at(at, 2)].reshape(2 * RANK, RANK))
        ltr_h[rows_at(at, 2 * RANK)] = w[0]
        ltr_l[rows_at(at, 2 * RANK)] = w[1]
        return product(split(q), w, dot)

    for level in range(DEPTH - 1):
        if level == 1:
            loads["ltu"].wait()

        def lift_two(m, level=level):
            qrow[PAIR[level + 1] + m] = jnp.concatenate(
                [lift(level, 2 * m), lift(level, 2 * m + 1)], 0
            )

        sweep(LEAVES >> (level + 2), lift_two, 16)
    loads["upt"].wait()

    e = [split(upt[0, k]) for k in range(LEVELS - 1)]
    zero = jnp.zeros((RANK, RANK), f32)

    def chain(first, count):
        out = [upt[0, first]]
        for k in range(first + 1, first + count):
            out.append(product(split(out[-1]), e[k], dot))
        return out

    t1, t2, t3 = chain(0, 3)
    wt1h[...], wt1l[...] = split(jnp.concatenate([t3, zero, t3, t1, t3, t2], 1))
    coef = lift(DEPTH - 1, 0)

    pending = []

    def exchange(phase, messages):
        first, levels = PHASES[phase]
        base = sum((1 << n) - 1 for _, n in PHASES[:phase])
        slot = sum(n for _, n in PHASES[:phase])
        for k in range(levels):
            send[slot + k] = messages[k]
        copies = []
        for p in sorted(range(1, 1 << levels), key=lambda p: -hops(p << first)):
            copy = pltpu.make_async_remote_copy(
                src_ref=send.at[slot + p.bit_length() - 1],
                dst_ref=recv.at[base + p - 1],
                send_sem=send_sem.at[base + p - 1],
                recv_sem=recv_sem.at[base + p - 1],
                device_id=(me ^ (p << first),),
                device_id_type=MESH,
            )
            copy.start()
            copies.append(copy)

        def receive():
            for copy in copies:
                copy.wait_recv()
            pending.extend(copies)
            sums = []
            for k in range(levels):
                parts = [recv[base + p - 1] for p in range(1 << k, 2 << k)]
                while len(parts) > 1:
                    parts = [a + b for a, b in zip(parts[::2], parts[1::2])]
                sums.append(parts[0])
            return sums

        return receive

    own = product(split(coef), (wt1h[...], wt1l[...]), dot)
    own = [own[:, 2 * RANK * k : 2 * RANK * (k + 1)] for k in range(3)]
    own[0] = own[0] + jnp.concatenate([half, coef], 1)
    pl.semaphore_wait(barrier, len(peers) + 2)
    receive = exchange(0, own)

    loads["pan"].wait()
    loads["area"].wait()
    halo_rows = jnp.zeros((5, 2 * LEAF), f32)

    def place(tile, slot):
        coords[slot] = tile[RHS:]
        coords[slot + 1] = pltpu.roll(tile[RHS:], LEAF, 1)
        high, rest = split(tile[:RHS].T)
        charge[pl.ds(slot, 2)] = jnp.concatenate([high, rest], 1).reshape(2, LEAF, 2 * RHS)

    def pack(p):
        at = rows_at(p, 2 * LEAF)
        where = jnp.concatenate([pan[:, at], halo_rows], 0)
        tile = jnp.concatenate([dens[:, at] * area[:, at], where], 0)
        if p in (0, 1, 14, 15):
            ends[p if p < 2 else p - 12] = tile
        place(tile, HALO + 2 * p)
        points[at, :] = where.T

    for p in (0, 1, 14, 15):
        pack(p)
    halos = []
    for at, (source, target, device) in enumerate(((2, 0, right), (0, 2, left))):
        copy = pltpu.make_async_remote_copy(
            src_ref=ends.at[pl.ds(source, 2)],
            dst_ref=halo.at[pl.ds(target, 2)],
            send_sem=halo_ssem.at[at],
            recv_sem=halo_rsem.at[at],
            device_id=(device,),
            device_id_type=MESH,
        )
        copy.start()
        halos.append(copy)
    for p in range(2, 14):
        pack(p)
    coords[NOLEAF] = jnp.zeros((8, 2 * LEAF), f32)
    coords[NOLEAF + 1] = jnp.zeros((8, 2 * LEAF), f32)
    charge[NOLEAF] = jnp.zeros((LEAF, 2 * RHS), bf16)

    u4, u5 = chain(3, 2)
    wt2h[...], wt2l[...] = split(jnp.concatenate([u5, zero, u5, u4], 1))
    v6, v7 = chain(5, 2)
    wt3h[...], wt3l[...] = split(jnp.concatenate([zero, v6, v7, zero], 1))
    loads["cpl"].wait()
    t4 = product(split(t3), e[3], dot)
    t5 = product(split(t3), split(u5), dot)
    t6 = product(split(t5), e[5], dot)
    t7 = product(split(t5), split(v7), dot)
    blank = jnp.zeros((2 * RANK, RANK), bf16)
    wk_h[:, rows_at(LEVELS, RANK)] = blank
    wk_l[:, rows_at(LEVELS, RANK)] = blank
    for k, t in enumerate((None, t1, t2, t3, t4, t5, t6, t7)):
        w = cpl[0, k] if t is None else product(split(t), split(cpl[0, k]), dot)
        wk_h[:, rows_at(k, RANK)], wk_l[:, rows_at(k, RANK)] = split(jnp.concatenate([w, w], 0))

    loads["lco"].wait()

    def couple(p):
        q = qrow[p]
        q = jnp.concatenate([q[RHS:], q[:RHS]], 0)
        w = split(lco[rows_at(p, 2)].reshape(2 * RANK, RANK))
        g = product(split(q), w, dot_t)
        gpair[p] = jnp.where(low, g[:RHS], g[RHS:])

    sweep(28, couple, 14)
    for p in range(28, 31):
        couple(p)

    top = rows_at(PAIR[4], 2 * RANK)
    gch[top] = ltr_h[top]
    gcl[top] = ltr_l[top]
    for level in range(DEPTH - 2, -1, -1):

        def compose(m, level=level):
            at = rows_at(PAIR[level] + m, 2 * RANK)
            up = rows_at(START[level + 1] + m, RANK)
            gch[at], gcl[at] = split(
                product((ltr_h[at], ltr_l[at]), (gch[up], gcl[up]), dot)
            )

        sweep(LEAVES >> (level + 1), compose, 16)

    sums = receive()
    tot = own[0] + (sums[0] + (sums[1] + sums[2]))
    coef = tot[:, :RANK]
    early = [s[:, RANK:] for s in sums]
    own = product(split(coef), (wt2h[...], wt2l[...]), dot)
    own = [own[:, 2 * RANK * k : 2 * RANK * (k + 1)] for k in range(2)]
    own[0] = own[0] + jnp.concatenate([half, coef], 1)
    receive = exchange(1, own)

    hpair[PAIR[4]] = gpair[PAIR[4]]

    for level in range(DEPTH - 2, -1, -1):

        def lower_two(m, level=level):
            parent = hpair[PAIR[level + 1] + m]
            for c in range(2):
                at = PAIR[level] + 2 * m + c
                w = (ltr_h[rows_at(at, 2 * RANK)], ltr_l[rows_at(at, 2 * RANK)])
                h = split(parent[:, RANK * c : RANK * (c + 1)])
                hpair[at] = gpair[at] + product(h, w, dot_t)

        sweep(LEAVES >> (level + 2), lower_two, 16)

    def far_leaf(p):
        h = hpair[p]
        h = jnp.concatenate([h[:, :RANK], h[:, RANK:]], 0)
        w = (bas_h[rows_at(p, 2 * LEAF)], bas_l[rows_at(p, 2 * LEAF)])
        far = product(split(h), w, dot_t)
        acc[:, rows_at(p, 2 * LEAF)] = jnp.where(low, far[:RHS], far[RHS:])

    sweep(LEAVES // 2, far_leaf, 16)

    loads["off"].wait()
    loads["cnt"].wait()
    for copy in halos:
        copy.wait()
    for end, slot, edge in ((0, 0, 0), (2, HALO + LEAVES, NODES - 1)):
        keep = jnp.where(me == edge, 0.0, 1.0)
        for t in range(2):
            place(halo[end + t] * keep, slot + 2 * t)

    def near_leaf(i):
        at = rows_at(i, LEAF)
        tx, ty, tz = (jnp.broadcast_to(points[at, c : c + 1], (LEAF, 2 * LEAF)) for c in range(3))
        count = cnt_ref[i]
        kernels, charges = [], []
        for t in range(NNEAR // 2):
            j = [
                jnp.where(s < count, off_ref[s, i] + (i + HALO), NOLEAF)
                for s in (2 * t, 2 * t + 1)
            ]
            charges += [charge[j[0]], charge[j[1]]]
            c = jnp.where(low, coords[j[0]], coords[j[1] ^ 1])
            dx = tx - c[0:1]
            dy = ty - c[1:2]
            dz = tz - c[2:3]
            kernels.append(lax.rsqrt(dx * dx + dy * dy + (dz * dz + softening)))
        high, rest = split(jnp.concatenate(kernels, 1))
        both = dot(jnp.concatenate([high, rest], 0), jnp.concatenate(charges, 0))
        column[at, :] = both[:LEAF] + both[LEAF:]

    def near(p):
        near_leaf(2 * p)
        near_leaf(2 * p + 1)

    def near_fold(p):
        at = rows_at(p, 2 * LEAF)
        tile = column[at, :].T
        acc[:, at] = acc[:, at] + (tile[:RHS] + tile[RHS:])

    def near_some(first, last):
        sweep(last - first, lambda p: near(p + first), 4)

    near_some(0, 8)

    sums = receive()
    tot = own[0] + (sums[0] + sums[1])
    coef = tot[:, :RANK]
    early += [s[:, RANK:] for s in sums]
    own = product(split(coef), (wt3h[...], wt3l[...]), dot)
    own = [jnp.concatenate([coef, half], 1), own[:, : 2 * RANK], own[:, 2 * RANK :]]
    receive = exchange(2, own)

    local = jnp.zeros((RHS, 2 * RANK), f32)
    for k in range(5):
        w = (wk_h[:, rows_at(k, RANK)], wk_l[:, rows_at(k, RANK)])
        local = local + product(split(early[k]), w, dot_t)

    def compose_leaf(p):
        pair = []
        for i in (2 * p, 2 * p + 1):
            at = rows_at(i, LEAF)
            pair.append(product((bas_h[at], bas_l[at]), (gch[at], gcl[at]), dot))
        high, rest = split(jnp.concatenate(pair, 0).T)
        dt[:, rows_at(p, 2 * LEAF)] = jnp.concatenate([high, rest], 0)

    sweep(LEAVES // 2, compose_leaf, 8)
    near_some(8, 16)
    for p in range(LEAVES // 2):
        near_fold(p)

    s5, s6, s7 = receive()
    tail = split(jnp.concatenate([s5 + s6, s7], 1))
    w = (wk_h[:, 5 * RANK :], wk_l[:, 5 * RANK :])
    for copy in pending:
        copy.wait_send()
    high, rest = split(local + product(tail, w, dot_t))
    rest = jnp.where(low, rest.astype(f32), 0.0).astype(bf16)
    local = jnp.concatenate([high, rest], 0)
    for b in range(4):
        at = rows_at(b, 512)
        far = dot(local, dt[:, at])
        out_ref[:, at] = acc[:, at] + (far[:RHS] + far[RHS:])


def per_device(
    densities, panels, areas, near_offsets, near_count,
    leaf_basis, local_trans, local_coupling, up_trans, coupling,
):
    hbm = pl.BlockSpec(memory_space=pltpu.HBM)
    nlocal = 2 * LEAVES - 2
    npeers = sum((1 << n) - 1 for _, n in PHASES)
    vm = pltpu.VMEM
    scratch = [
        pltpu.SMEM((NNEAR, LEAVES), jnp.int32),
        pltpu.SMEM((LEAVES,), jnp.int32),
        vm((RHS, SPAN), f32),
        vm((3, SPAN), f32),
        vm((1, SPAN), f32),
        vm((LEAVES, LEAF, RANK), f32),
        vm((nlocal, RANK, RANK), f32),
        vm((nlocal, RANK, RANK), f32),
        vm((1, LEVELS, RANK, RANK), f32),
        vm((1, LEVELS, RANK, RANK), f32),
        vm((SPAN, RANK), bf16),
        vm((SPAN, RANK), bf16),
        vm((nlocal * RANK, RANK), bf16),
        vm((nlocal * RANK, RANK), bf16),
        vm((nlocal * RANK, RANK), bf16),
        vm((nlocal * RANK, RANK), bf16),
        vm((2 * RANK, SPAN), bf16),
        vm((NOLEAF + 2, 8, 2 * LEAF), f32),
        vm((NOLEAF + 1, LEAF, 2 * RHS), bf16),
        vm((4, RHS + 8, 2 * LEAF), f32),
        vm((4, RHS + 8, 2 * LEAF), f32),
        vm((SPAN, 2 * RHS), f32),
        vm((SPAN, 8), f32),
        vm((nlocal // 2, 2 * RHS, RANK), f32),
        vm((nlocal // 2, RHS, 2 * RANK), f32),
        vm((nlocal // 2, RHS, 2 * RANK), f32),
        vm((RHS, SPAN), f32),
        vm((RANK, 6 * RANK), bf16),
        vm((RANK, 6 * RANK), bf16),
        vm((RANK, 4 * RANK), bf16),
        vm((RANK, 4 * RANK), bf16),
        vm((RANK, 4 * RANK), bf16),
        vm((RANK, 4 * RANK), bf16),
        vm((2 * RANK, 9 * RANK), bf16),
        vm((2 * RANK, 9 * RANK), bf16),
        vm((LEVELS, RHS, 2 * RANK), f32),
        vm((npeers, RHS, 2 * RANK), f32),
        pltpu.SemaphoreType.DMA((11,)),
        pltpu.SemaphoreType.DMA((npeers,)),
        pltpu.SemaphoreType.DMA((npeers,)),
        pltpu.SemaphoreType.DMA((2,)),
        pltpu.SemaphoreType.DMA((2,)),
    ]
    return pl.pallas_call(
        kernel,
        out_shape=jax.ShapeDtypeStruct((RHS, SPAN), f32),
        in_specs=[hbm] * 10,
        out_specs=pl.BlockSpec(memory_space=pltpu.VMEM),
        scratch_shapes=scratch,
        compiler_params=pltpu.CompilerParams(
            collective_id=0, has_side_effects=True, vmem_limit_bytes=40 * 1024 * 1024
        ),
    )(*[
        pltpu.with_memory_space_constraint(v, pltpu.HBM)
        for v in (densities, panels, areas.reshape(1, SPAN), near_offsets.T, near_count,
        leaf_basis, local_trans, local_coupling, up_trans, coupling)
    ])


def solution(mesh):
    return jax.shard_map(
        per_device,
        mesh=mesh,
        in_specs=(
            P(None, "leaf"),
            P(None, "leaf"),
            P("leaf"),
            P("leaf", None),
            P("leaf"),
            P("leaf", None, None),
            P("leaf", None, None),
            P("leaf", None, None),
            P("leaf", None, None, None),
            P("leaf", None, None, None),
        ),
        out_specs=P(None, "leaf"),
        check_vma=False,
    )
```
